256 devices in a mesh: wide: 32 (over y, z), narrow: 8 (over x, core).
Axes of the slice: x: 4, y: 4, z: 8, core: 2. Of those that a mesh axis runs over, the one named last changes fastest.
Arguments:
- grad_out: bfloat16 [512, 28672], P('wide', 'narrow'), may hold values from -1.5 to 1.5
- inputs: bfloat16 [512, 8192], P('narrow', 'wide'), may hold values from -1.5 to 1.5
- q_grad: bfloat16 [28672, 28672], P('narrow', 'wide'), may hold values from -0.03125 to 0.03125
- q_input: bfloat16 [8192, 8192], P('wide', 'narrow'), may hold values from -0.0625 to 0.0625
- eig_corr: bfloat16 [28672, 8192], P('wide', 'narrow'), may hold values from 0.1 to 5, as said below
- example_ids: int32 [512], replicated, may hold values from 0 to 1, never falling along the last dimension, each value on 1 to 384 neighbouring positions
Outputs:
- precond: bfloat16 [2, 28672, 8192], P(None, 'wide', 'narrow')
- scores: float32 [2], replicated
The draws below stay inside these ranges and needn't reach their ends.
Inputs may be any that keep to these rules, and one draw needn't show every extreme that they name: `example_ids`: each example's tokens stand together, examples in increasing order. `eig_corr`: Positive.
All inputs are finite; a program needn't handle non-finite values.
Results may differ from the reference program's by a relative error of at most 0.0058.
Values may be sent and summed in bfloat16 or wider, within the bound.
No kernel may reach another device: no remote copies, remote signals or barrier semaphores. Data moves between devices by JAX's collectives and lax.ppermute only.
A program may use at most 64 MiB of HBM per device.

```python
import math
import jax
import jax.numpy as jnp
import numpy as np
from jax import lax

DOUT = 28672
DIN = 8192
EXAMPLES = 2
SEQ = 256
TOKENS = 512


def draw_eig_corr(key, part):
    key = jax.random.fold_in(key, 7)
    rows = lax.broadcasted_iota(jnp.float32, (DOUT, DIN), 0) / DOUT
    base = jnp.exp(jax.random.uniform(key, (DOUT, DIN), jnp.float32, math.log(0.5), math.log(5.0)))
    return (base * jnp.exp(-1.2 * rows)).astype(jnp.bfloat16)


def level_of(stream_key, shape, cuts, least, top_value):
    def one(position, shards_of):
        steps = jax.random.uniform(jax.random.fold_in(jax.random.fold_in(stream_key, 6), position), (shards_of,), jnp.float32, least / len(cuts), top_value / len(cuts))
        return jnp.repeat(jnp.exp(steps), shape[position] // shards_of).reshape((-1,) + (1,) * (len(shape) - position - 1))

    gain = one(*cuts[0])
    for cut in cuts[1:]:
        gain = gain * one(*cut)
    return gain


def profile(amount, total, bound, lean):
    loads = [(1 << 20) // math.isqrt(rank ** lean) + 1 for rank in range(2, amount + 1)]
    surplus, given = total - bound - (amount - 1), [1] * (amount - 1)
    while surplus > 0:
        free = [i for i in range(amount - 1) if given[i] < bound]
        pool, budget = sum([loads[i] for i in free]), surplus
        for i in free:
            addition = min(bound - given[i], max(1, budget * loads[i] // pool), surplus)
            given[i] = given[i] + addition
            surplus = surplus - addition
    return np.array([bound] + given)


def ragged(own_key, number_of, total, most, lean):
    if number_of == 2:
        one = jax.random.randint(own_key, (), max(1, total - most), min(most, total - 1) + 1)
        return jnp.stack([one, total - one])
    tallies = jnp.asarray(profile(number_of, total, most, lean), jnp.int32)
    couples = (number_of - 1) // 2
    source_of, receiver = tallies[1:1 + 2 * couples:2], tallies[2:2 + 2 * couples:2]
    margin = jnp.minimum(source_of - 1, most - receiver)
    moved = jax.random.randint(jax.random.fold_in(own_key, 1), (couples,), 0, 1 << 20) % (margin + 1)
    tallies = tallies.at[1:1 + 2 * couples:2].set(source_of - moved).at[2:2 + 2 * couples:2].set(receiver + moved)
    return tallies[jax.random.permutation(jax.random.fold_in(own_key, 2), number_of)]


def scatter_about(key, dims, deviation, reach, shards=(), kind=jnp.bfloat16):
    result = deviation * jax.random.normal(key, dims, jnp.float32)
    if shards:
        result = result * level_of(key, dims, shards, -0.22, 0.18)
    return jnp.clip(result, -reach, reach).astype(kind)


def setup_inputs(seed: int = 0) -> dict:
    splits = jax.random.split(jax.random.key(seed), 7)
    grad_out = scatter_about(splits[0], (TOKENS, DOUT), 0.25, 1.5, ((0, 32), (1, 8)))
    inputs = scatter_about(splits[1], (TOKENS, DIN), 0.25, 1.5, ((0, 8), (1, 32)))
    q_grad = scatter_about(splits[2], (DOUT, DOUT), DOUT ** -0.5, 0.03125, ((0, 8), (1, 32)))
    q_input = scatter_about(splits[3], (DIN, DIN), DIN ** -0.5, 0.0625, ((0, 32), (1, 8)))
    eig_corr = draw_eig_corr(jax.random.fold_in(splits[6], 71), 0)
    example_ids = jnp.searchsorted(jnp.cumsum(ragged(splits[5], EXAMPLES, TOKENS, SEQ + SEQ // 2, 0)), jnp.arange(TOKENS), side="right").astype(jnp.int32)
    return {"grad_out": grad_out, "inputs": inputs, "q_grad": q_grad, "q_input": q_input, "eig_corr": eig_corr, "example_ids": example_ids}


def reference(grad_out, inputs, q_grad, q_input, eig_corr, example_ids):
    grad_rot = jnp.dot(grad_out, q_grad, preferred_element_type=jnp.float32).astype(jnp.bfloat16)
    input_rot = jnp.dot(inputs, q_input, preferred_element_type=jnp.float32).astype(jnp.bfloat16)
    corrected = eig_corr.astype(jnp.float32)

    def one_example(index):
        weights = (example_ids == index).astype(jnp.bfloat16)[:, None]
        masked = grad_rot * weights
        blocks = jnp.dot(masked.T, input_rot, preferred_element_type=jnp.float32)
        scaled = blocks / corrected
        return scaled.astype(jnp.bfloat16), jnp.sum(blocks * scaled)

    precond, totals = lax.map(one_example, jnp.arange(EXAMPLES, dtype=jnp.int32))
    scores = totals / jnp.float32(DOUT * DIN)
    return precond, scores
```

```python
import jax
import jax.numpy as jnp
from jax import lax
from jax.sharding import Mesh, PartitionSpec as P

DOUT = 28672
DIN = 8192
EXAMPLES = 2
NY, NZ, NX, NC = 4, 8, 4, 2
SIZES = {"y": NY, "z": NZ, "x": NX, "c": NC}
CUT = 1792
BF = jnp.bfloat16
F32 = jnp.float32


def shift(a, axis, k):
    n = SIZES[axis]
    return lax.ppermute(a, axis, [(i, (i + k) % n) for i in range(n)])


def trade(a, axes):
    return lax.all_to_all(a, axes, 0, 0)


def spread(a, axes, n):
    return trade(jnp.broadcast_to(a[None], (n,) + a.shape), axes)


def dot(a, b):
    return jnp.dot(a, b, preferred_element_type=F32)


def rotate_inputs(inputs, q_input):
    whole = spread(inputs, ("x", "c"), NX * NC).reshape(512, 256)
    part = dot(whole, q_input).astype(BF)
    part = trade(part.reshape(NY, 128, 1024), "y").astype(F32).sum(0).astype(BF)
    part = trade(part.reshape(NZ, 16, 1024), "z").astype(F32).sum(0).astype(BF)
    part = spread(part, "z", NZ).reshape(128, 1024)
    return spread(part, "y", NY).reshape(512, 1024)


def order(example_ids):
    y, z, c = lax.axis_index("y"), lax.axis_index("z"), lax.axis_index("c")
    r = lax.broadcasted_iota(jnp.int32, (512, 512), 0)
    t = lax.broadcasted_iota(jnp.int32, (512, 512), 1)
    half, yo, zo, s = r // 256, (r // 128) % 2, (r // 16) % 8, r % 16
    yo = 2 * ((half + c) % 2) + yo
    token = ((y + yo) % NY) * 128 + ((z + zo) % NZ) * 16 + s
    pick = token == t
    labels = jnp.arange(EXAMPLES, dtype=jnp.int32)[:, None, None]
    return (pick[None] & (example_ids[None, None, :] == labels)).astype(BF)


def rotate_grads(grad_out, q_grad):
    a, b = grad_out[:, :CUT], grad_out[:, CUT:]
    qa, qb = q_grad[:CUT], q_grad[CUT:]
    up = down = a
    ups, downs = [], []
    for _ in range(3):
        up, down = shift(up, "z", 1), shift(down, "z", -1)
        ups.append(up)
        downs.append(down)
    h = CUT // 2
    far = jnp.concatenate([shift(up[:, :h], "z", 1), shift(down[:, h:], "z", -1)], 1)
    column = jnp.concatenate([a] + downs + [far] + ups[::-1], 0)
    rows = [column] + [shift(column, "y", k) for k in (3, 2, 1)]
    pa = [dot(row, qa).reshape(NZ, 16, 896) for row in rows]
    own = jnp.concatenate([b] + [shift(b, "y", k) for k in (3, 2, 1)], 0)
    pb = [None] * NZ
    pb[0] = dot(own, qb)
    up = down = own
    for k in range(1, 4):
        up, down = shift(up, "z", 1), shift(down, "z", -1)
        pb[k], pb[NZ - k] = dot(down, qb), dot(up, qb)
    h = (3584 - CUT) // 2
    far = jnp.concatenate([shift(up[:, :h], "z", 1), shift(down[:, h:], "z", -1)], 1)
    pb[4] = dot(far, qb)
    pb = jnp.stack([p.reshape(NY, 16, 896) for p in pb], 1)
    total = (jnp.stack(pa, 0) + pb).reshape(2, 256, 896)
    first = lax.axis_index("c") == 0
    mine = jnp.where(first, total[0], total[1])
    other = jnp.where(first, total[1], total[0])
    mine = mine + shift(other, "c", 1)
    mine = trade(mine.reshape(NX, 64, 896).astype(BF), "x").astype(F32).sum(0).astype(BF)
    mine = spread(mine, "x", NX).reshape(256, 896)
    return jnp.concatenate([mine, shift(mine, "c", 1)], 0)


def local(grad_out, inputs, q_grad, q_input, eig_corr, example_ids):
    input_rot = rotate_inputs(inputs, q_input)
    picked = jnp.einsum("ert,ti->eri", order(example_ids), input_rot, preferred_element_type=F32).astype(BF)
    grad_rot = rotate_grads(grad_out, q_grad)
    blocks = jnp.einsum("ro,eri->eoi", grad_rot, picked, preferred_element_type=F32)
    scaled = blocks / eig_corr.astype(F32)[None]
    precond = scaled.astype(BF)
    sums = jnp.sum(blocks * scaled, axis=(1, 2))
    sums = jnp.broadcast_to(sums[:, None], (EXAMPLES, 128))
    sums = spread(sums, ("x", "c"), NX * NC).sum(0)
    sums = spread(sums, ("y", "z"), NY * NZ).sum(0)
    scores = sums[:, 0] / F32(DOUT * DIN)
    return precond, scores


def solution(mesh):
    fine = Mesh(mesh.devices.reshape(NY, NZ, NX, NC), ("y", "z", "x", "c"))
    wide, narrow = ("y", "z"), ("x", "c")
    return jax.shard_map(
        local,
        mesh=fine,
        in_specs=(P(wide, narrow), P(narrow, wide), P(narrow, wide), P(wide, narrow), P(wide, narrow), P()),
        out_specs=(P(None, wide, narrow), P()),
        check_vma=False,
    )
```

```python
import jax
import jax.numpy as jnp
from jax import lax
from jax.sharding import Mesh, PartitionSpec as P

DOUT = 28672
DIN = 8192
EXAMPLES = 2
TOKENS = 512
NY, NZ, NX, NC = 4, 8, 4, 2
SIZES = {"y": NY, "z": NZ, "x": NX, "c": NC}
BF = jnp.bfloat16
F32 = jnp.float32


def shift(a, axis, k):
    n = SIZES[axis]
    return lax.ppermute(a, axis, [(i, (i + k) % n) for i in range(n)])


def trade(a, axes):
    return lax.all_to_all(a, axes, 0, 0)


def spread(a, axes, n):
    return trade(jnp.broadcast_to(a[None], (n,) + a.shape), axes)


def dot(a, b):
    return jnp.dot(a, b, preferred_element_type=F32)


def after(a, *others):
    return lax.optimization_barrier((a,) + others)[0]


def order(example_ids):
    y, z, x, c = (lax.axis_index(a) for a in ("y", "z", "x", "c"))
    r = lax.broadcasted_iota(jnp.int32, (TOKENS, 1), 0)
    early = r < 448
    half = jnp.where(early, r // 224, (r - 448) // 32)
    at = 56 * (((r % 224) // 56 + x) % NX) + r % 56
    n = at // 32
    zo = jnp.where(early, jnp.where(n % 2 == 1, (n + 1) // 2, (8 - n // 2) % 8), 4)
    w = jnp.where(early, at % 32, r % 32)
    yo = 2 * ((half + c) % 2) + w // 16
    token = ((y + yo) % NY) * 128 + ((z + zo) % NZ) * 16 + w % 16
    pick = token == lax.broadcasted_iota(jnp.int32, (TOKENS, TOKENS), 1)
    labels = jnp.arange(EXAMPLES, dtype=jnp.int32)[:, None, None]
    return (pick[None] & (example_ids[None, None, :] == labels)).astype(BF)


def halves(total):
    total = total.reshape(-1, 2, 32, 896)
    first = lax.axis_index("c") == 0
    mine = jnp.where(first, total[:, 0], total[:, 1])
    other = jnp.where(first, total[:, 1], total[:, 0])
    return (mine + shift(other, "c", 1)).reshape(-1, 896).astype(BF)


def both(mine):
    return jnp.concatenate([mine, shift(mine, "c", 1)], 0)


def local(grad_out, inputs, q_grad, q_input, eig_corr, example_ids):
    x = lax.axis_index("x")
    whole = spread(inputs, ("x", "c"), NX * NC)
    own = jnp.concatenate([grad_out] + [shift(grad_out, "y", k) for k in (3, 2, 1)], 0)

    part = dot(whole.reshape(TOKENS, 256), q_input).astype(BF)
    up, down = shift(own, "z", 1), shift(own, "z", -1)
    part = trade(part.reshape(NY, 128, 1024), "y").astype(F32).sum(0).astype(BF)
    total = [dot(own, q_grad)]

    total += [dot(down, q_grad), dot(up, q_grad)]
    up, down, part = lax.optimization_barrier((up, down, part))
    up, down = shift(up, "z", 1), shift(down, "z", -1)
    part = trade(part.reshape(NZ, 16, 1024), "z").astype(F32).sum(0).astype(BF)

    total += [dot(down, q_grad), dot(up, q_grad)]
    up, down, part = lax.optimization_barrier((up, down, part))
    up, down = shift(up, "z", 1), shift(down, "z", -1)
    part = spread(part, "z", NZ).reshape(128, 1024)

    total += [dot(down, q_grad), dot(up, q_grad)]
    up, down, part = lax.optimization_barrier((up, down, part))
    up, down = shift(up[:, :1792], "z", 1), shift(down[:, 1792:], "z", -1)
    input_rot = spread(part, "y", NY).reshape(TOKENS, 1024)

    mine = halves(jnp.concatenate(total, 0)).reshape(NX, 56, 896)
    quarter = [lax.dynamic_index_in_dim(mine, (x + k) % NX, 0, False) for k in range(NX)]
    part = quarter[0].astype(F32)
    for k in range(1, NX):
        part = part + shift(quarter[k], "x", k).astype(F32)
    part = part.astype(BF)
    early = both(jnp.concatenate([part] + [shift(part, "x", NX - k) for k in range(1, NX)], 0))

    mine = halves(dot(jnp.concatenate([up, down], 1), q_grad))
    part = mine.astype(F32)
    for k in range(1, NX):
        part = part + shift(mine, "x", k).astype(F32)
    late = both(part.astype(BF))
    grad_rot = jnp.concatenate([early, late], 0)

    picked = jnp.einsum("ert,ti->eri", order(example_ids), input_rot, preferred_element_type=F32).astype(BF)
    blocks = jnp.einsum("ro,eri->eoi", grad_rot, picked, preferred_element_type=F32)
    scaled = blocks / eig_corr.astype(F32)[None]
    precond = scaled.astype(BF)
    sums = jnp.sum(blocks * scaled, axis=(1, 2))
    sums = jnp.broadcast_to(sums[:, None], (EXAMPLES, 128))
    sums = spread(sums, ("x", "c"), NX * NC).sum(0)
    sums = spread(sums, ("y", "z"), NY * NZ).sum(0)
    scores = sums[:, 0] / F32(DOUT * DIN)
    return precond, scores


def solution(mesh):
    fine = Mesh(mesh.devices.reshape(NY, NZ, NX, NC), ("y", "z", "x", "c"))
    wide, narrow = ("y", "z"), ("x", "c")
    return jax.shard_map(
        local,
        mesh=fine,
        in_specs=(P(wide, narrow), P(narrow, wide), P(narrow, wide), P(wide, narrow), P(wide, narrow), P()),
        out_specs=(P(None, wide, narrow), P()),
        check_vma=False,
    )
```

```python
import jax
import jax.numpy as jnp
from jax import lax
from jax.sharding import Mesh, PartitionSpec as P

DOUT = 28672
DIN = 8192
EXAMPLES = 2
TOKENS = 512
NY, NZ, NX, NC = 4, 8, 4, 2
SIZES = {"y": NY, "z": NZ, "x": NX, "c": NC}
BF = jnp.bfloat16
F32 = jnp.float32


def shift(a, axis, k):
    n = SIZES[axis]
    return lax.ppermute(a, axis, [(i, (i + k) % n) for i in range(n)])


def trade(a, axes):
    return lax.all_to_all(a, axes, 0, 0)


def spread(a, axes, n):
    return trade(jnp.broadcast_to(a[None], (n,) + a.shape), axes)


def dot(a, b):
    return jnp.dot(a, b, preferred_element_type=F32)


def order(example_ids):
    y, z, c = (lax.axis_index(a) for a in ("y", "z", "c"))
    r = lax.broadcasted_iota(jnp.int32, (TOKENS, 1), 0)
    middle = (r >= 128) & (r < 384)
    half = jnp.where(middle, (r - 128) // 128, (r // 64) % 2)
    yo = jnp.where(middle, jnp.where((r // 64) % 2 == 0, 1, 3), jnp.where(r < 128, 0, 2))
    zo = 4 * ((half + c) % 2) + (r // 16) % 4
    token = ((y + yo) % NY) * 128 + ((z + zo) % NZ) * 16 + r % 16
    pick = token == lax.broadcasted_iota(jnp.int32, (TOKENS, TOKENS), 1)
    labels = jnp.arange(EXAMPLES, dtype=jnp.int32)[:, None, None]
    return (pick[None] & (example_ids[None, None, :] == labels)).astype(BF)


def add_narrow(total):
    total = total.reshape(-1, 2, 64, 896)
    first = lax.axis_index("c") == 0
    mine = jnp.where(first, total[:, 0], total[:, 1])
    other = jnp.where(first, total[:, 1], total[:, 0])
    mine = (mine + shift(other, "c", 1)).reshape(-1, 896).astype(BF)
    part = mine.astype(F32)
    for k in range(1, NX):
        part = part + shift(mine, "x", k).astype(F32)
    part = part.astype(BF)
    return jnp.concatenate([part, shift(part, "c", 1)], 0)


def local(grad_out, inputs, q_grad, q_input, eig_corr, example_ids):
    whole = spread(inputs, ("x", "c"), NX * NC)
    up, down = shift(grad_out, "z", 1), shift(grad_out, "z", -1)
    ups, downs = [up], [down]

    part = dot(whole.reshape(TOKENS, 256), q_input).astype(BF)
    up, down, part = lax.optimization_barrier((up, down, part))
    part = trade(part.reshape(NY, 128, 1024), "y").astype(F32).sum(0).astype(BF)
    for _ in range(2):
        up, down = shift(up, "z", 1), shift(down, "z", -1)
        ups.append(up)
        downs.append(down)
    far = jnp.concatenate([shift(up[:, :1792], "z", 1), shift(down[:, 1792:], "z", -1)], 1)
    own = jnp.concatenate([grad_out] + downs + [far] + ups[::-1], 0)
    own, part = lax.optimization_barrier((own, part))

    up, down = shift(own, "y", 1), shift(own, "y", -1)
    part = trade(part.reshape(NZ, 16, 1024), "z").astype(F32).sum(0).astype(BF)
    rot = [add_narrow(dot(own, q_grad))]
    up, down, part = lax.optimization_barrier((up, down, part))

    far = jnp.concatenate([shift(up[:, :1792], "y", 1), shift(down[:, 1792:], "y", -1)], 1)
    part = spread(part, "z", NZ).reshape(128, 1024)
    up, down, part = lax.optimization_barrier((up, down, part))
    rot += [add_narrow(dot(jnp.concatenate([down, up], 0), q_grad))]

    input_rot = spread(part, "y", NY).reshape(TOKENS, 1024)
    rot += [add_narrow(dot(far, q_grad))]
    grad_rot = jnp.concatenate(rot, 0)

    picked = jnp.einsum("ert,ti->eri", order(example_ids), input_rot, preferred_element_type=F32).astype(BF)
    blocks = jnp.einsum("ro,eri->eoi", grad_rot, picked, preferred_element_type=F32)
    scaled = blocks / eig_corr.astype(F32)[None]
    precond = scaled.astype(BF)
    sums = jnp.sum(blocks * scaled, axis=(1, 2))
    sums = jnp.broadcast_to(sums[:, None], (EXAMPLES, 128))
    sums = spread(sums, ("x", "c"), NX * NC).sum(0)
    sums = spread(sums, ("y", "z"), NY * NZ).sum(0)
    scores = sums[:, 0] / F32(DOUT * DIN)
    return precond, scores


def solution(mesh):
    fine = Mesh(mesh.devices.reshape(NY, NZ, NX, NC), ("y", "z", "x", "c"))
    wide, narrow = ("y", "z"), ("x", "c")
    return jax.shard_map(
        local,
        mesh=fine,
        in_specs=(P(wide, narrow), P(narrow, wide), P(narrow, wide), P(wide, narrow), P(wide, narrow), P()),
        out_specs=(P(None, wide, narrow), P()),
        check_vma=False,
    )
```

```python
import jax
import jax.numpy as jnp
from jax import lax
from jax.experimental import pallas as pl
from jax.experimental.pallas import tpu as pltpu
from jax.sharding import Mesh, PartitionSpec as P

DOUT = 28672
DIN = 8192
EXAMPLES = 2
TOKENS = 512
ROWS, COLS = 896, 1024
NY, NZ, NX, NC = 4, 8, 4, 2
SIZES = {"y": NY, "z": NZ, "x": NX, "c": NC}
BF = jnp.bfloat16
F32 = jnp.float32


def shift(a, axis, k):
    n = SIZES[axis]
    return lax.ppermute(a, axis, [(i, (i + k) % n) for i in range(n)])


def trade(a, axes):
    return lax.all_to_all(a, axes, 0, 0)


def spread(a, axes, n):
    return trade(jnp.broadcast_to(a[None], (n,) + a.shape), axes)


def dot(a, b):
    return jnp.dot(a, b, preferred_element_type=F32)


def together(*arrays):
    return lax.optimization_barrier(arrays)


def grad_tokens():
    y, z, c = (lax.axis_index(a) for a in ("y", "z", "c"))
    r = lax.broadcasted_iota(jnp.int32, (TOKENS, 1), 0)
    early = r < 384
    half = jnp.where(early, r // 192, (r // 64) % 2)
    chunk = (r // 64) % 3
    yo = jnp.where(early, jnp.where(chunk == 2, 3, chunk), 2)
    zo = 4 * ((half + c) % 2) + (r // 16) % 4
    return ((y + yo) % NY) * 128 + ((z + zo) % NZ) * 16 + r % 16


def input_tokens():
    x, c = lax.axis_index("x"), lax.axis_index("c")
    r = lax.broadcasted_iota(jnp.int32, (1, TOKENS), 1)
    return 128 * ((x + r // 64) % NX) + 64 * ((c + r // 256) % NC) + r % 64


def order(example_ids):
    rows = grad_tokens()
    pick = rows == input_tokens()
    second = rows >= jnp.sum((example_ids == 0).astype(jnp.int32))
    return jnp.stack([pick & ~second, pick & second]).astype(BF)


def project_kernel(count, parts, core_ref, *refs):
    lhs, q_refs = refs[: count * parts], refs[count * parts : count * parts + parts]
    mine_ref, other_ref, acc_ref = refs[count * parts + parts :]
    step = pl.program_id(0)

    @pl.when(step == 0)
    def _():
        acc_ref[...] = jnp.zeros_like(acc_ref)

    for i in range(count):
        for j in range(parts):
            acc_ref[i] += dot(lhs[i * parts + j][...], q_refs[j][...])

    @pl.when(step == pl.num_programs(0) - 1)
    def _():
        here = pl.multiple_of(core_ref[0] * 64, 64)
        there = pl.multiple_of(64 - core_ref[0] * 64, 64)
        for i in range(count):
            mine_ref[i] = acc_ref[i, pl.ds(here, 64), :]
            other_ref[i] = acc_ref[i, pl.ds(there, 64), :]


def project(chunks, q_grad, weight):
    count, parts = len(chunks), len(chunks[0])
    steps = 7
    depth = q_grad.shape[0] // parts // steps
    core = lax.axis_index("c").astype(jnp.int32).reshape(1)
    half = jax.ShapeDtypeStruct((count, 64, ROWS), F32)
    return pl.pallas_call(
        lambda *refs: project_kernel(count, parts, *refs),
        grid_spec=pltpu.PrefetchScalarGridSpec(
            num_scalar_prefetch=1,
            grid=(steps,),
            in_specs=[pl.BlockSpec((128, depth), lambda k, _: (0, k))] * (count * parts)
            + [pl.BlockSpec((depth, ROWS), lambda k, _, j=j: (j * steps + k, 0)) for j in range(parts)],
            out_specs=[pl.BlockSpec((count, 64, ROWS), lambda k, _: (0, 0, 0))] * 2,
            scratch_shapes=[pltpu.VMEM((count, 128, ROWS), F32)],
        ),
        out_shape=[half, half],
        compiler_params=pltpu.CompilerParams(vmem_limit_bytes=48 * 1024 * 1024),
        cost_estimate=pl.CostEstimate(
            flops=weight * 256 * count * q_grad.size, bytes_accessed=weight * 2 * q_grad.size, transcendentals=0
        ),
    )(core, *(part for chunk in chunks for part in chunk), *([q_grad] * parts))


def add_core(halves):
    mine, other = halves
    return (mine + shift(other, "c", 1)).reshape(-1, ROWS).astype(BF)


def add_chips(mine):
    part = mine.astype(F32)
    for k in range(1, NX):
        part = part + shift(mine, "x", k).astype(F32)
    return part.astype(BF)


def both(part):
    return jnp.concatenate([part, shift(part, "c", 1)], 0)


def finish_kernel(g_ref, a_ref, eig_ref, out_ref, sum_ref, acc_ref):
    step = pl.program_id(0)

    @pl.when(step == 0)
    def _():
        acc_ref[...] = jnp.zeros_like(acc_ref)

    scale = 1.0 / eig_ref[...].astype(F32)
    for e in range(EXAMPLES):
        blocks = lax.dot_general(g_ref[...], a_ref[e], (((0,), (0,)), ((), ())), preferred_element_type=F32)
        scaled = blocks * scale
        out_ref[e] = scaled.astype(BF)
        acc_ref[e] += (blocks * scaled).reshape(-1, 8, COLS).sum(0)

    @pl.when(step == pl.num_programs(0) - 1)
    def _():
        lanes = acc_ref[...].sum(1)
        sum_ref[...] = sum(lanes[:, 128 * k : 128 * (k + 1)] for k in range(COLS // 128))


def finish(grad_rot, picked, eig_corr):
    tile = 128
    return pl.pallas_call(
        finish_kernel,
        grid=(ROWS // tile,),
        in_specs=[
            pl.BlockSpec((TOKENS, tile), lambda i: (0, i)),
            pl.BlockSpec((EXAMPLES, TOKENS, COLS), lambda i: (0, 0, 0)),
            pl.BlockSpec((tile, COLS), lambda i: (i, 0)),
        ],
        out_specs=[
            pl.BlockSpec((EXAMPLES, tile, COLS), lambda i: (0, i, 0)),
            pl.BlockSpec((EXAMPLES, 128), lambda i: (0, 0)),
        ],
        out_shape=[
            jax.ShapeDtypeStruct((EXAMPLES, ROWS, COLS), BF),
            jax.ShapeDtypeStruct((EXAMPLES, 128), F32),
        ],
        scratch_shapes=[pltpu.VMEM((EXAMPLES, 8, COLS), F32)],
        compiler_params=pltpu.CompilerParams(vmem_limit_bytes=24 * 1024 * 1024),
        cost_estimate=pl.CostEstimate(
            flops=4 * TOKENS * ROWS * COLS, bytes_accessed=8 * ROWS * COLS, transcendentals=0
        ),
    )(grad_rot, picked, eig_corr)


def local(grad_out, inputs, q_grad, q_input, eig_corr, example_ids):
    whole = jnp.concatenate([inputs] + [shift(inputs, "x", NX - k) for k in range(1, NX)], 0)
    up, down = shift(grad_out, "z", 1), shift(grad_out, "z", -1)
    ups, downs = [up], [down]
    whole = both(whole)

    part = dot(whole, q_input).astype(BF)
    up, down, part = together(up, down, part)
    part = trade(part.reshape(NY, 128, COLS), "y").astype(F32).sum(0).astype(BF)
    for _ in range(2):
        up, down = shift(up, "z", 1), shift(down, "z", -1)
        ups.append(up)
        downs.append(down)
    far = jnp.concatenate([shift(up[:, :1792], "z", 1), shift(down[:, 1792:], "z", -1)], 1)
    own = jnp.concatenate([grad_out] + downs + [far] + ups[::-1], 0)
    own, part = together(own, part)

    up, down = shift(own, "y", 1), shift(own, "y", -1)
    part = trade(part.reshape(NZ, 16, COLS), "z").astype(F32).sum(0).astype(BF)
    mine = add_core(project([[own]], q_grad, 8))
    up, down, part, mine = together(up, down, part, mine)

    far = [shift(up[:, :1792], "y", 1), shift(down[:, 1792:], "y", -1)]
    part = spread(part, "z", NZ).reshape(128, COLS)
    mine = jnp.concatenate([mine, add_core(project([[down], [up]], q_grad, 8))], 0)
    *far, part, mine = together(*far, part, mine)

    input_rot = spread(part, "y", NY).reshape(TOKENS, COLS)
    first = both(add_chips(mine))
    last = add_chips(add_core(project([far], q_grad, 8)))
    last, first, input_rot = together(last, first, input_rot)
    rot = [first, both(last)]

    picked = jnp.einsum("ert,ti->eri", order(example_ids), input_rot, preferred_element_type=F32).astype(BF)
    precond, sums = finish(jnp.concatenate(rot, 0), picked, eig_corr)
    sums = spread(sums, ("x", "c"), NX * NC).sum(0)
    sums = spread(sums, ("y", "z"), NY * NZ).sum(0)
    scores = sums.sum(1) / F32(DOUT * DIN)
    return precond, scores


def solution(mesh):
    fine = Mesh(mesh.devices.reshape(NY, NZ, NX, NC), ("y", "z", "x", "c"))
    wide, narrow = ("y", "z"), ("x", "c")
    return jax.shard_map(
        local,
        mesh=fine,
        in_specs=(P(wide, narrow), P(narrow, wide), P(narrow, wide), P(wide, narrow), P(wide, narrow), P()),
        out_specs=(P(None, wide, narrow), P()),
        check_vma=False,
    )
```

```python
import jax
import jax.numpy as jnp
from jax import lax
from jax.experimental import pallas as pl
from jax.experimental.pallas import tpu as pltpu
from jax.sharding import Mesh, PartitionSpec as P

DOUT = 28672
DIN = 8192
EXAMPLES = 2
TOKENS = 512
ROWS, COLS = 896, 1024
NY, NZ, NX, NC = 4, 8, 4, 2
SIZES = {"y": NY, "z": NZ, "x": NX, "c": NC}
BF = jnp.bfloat16
F32 = jnp.float32


def shift(a, axis, k):
    n = SIZES[axis]
    return lax.ppermute(a, axis, [(i, (i + k) % n) for i in range(n)])


def trade(a, axes):
    return lax.all_to_all(a, axes, 0, 0)


def spread(a, axes, n):
    return trade(jnp.broadcast_to(a[None], (n,) + a.shape), axes)


def dot(a, b):
    return jnp.dot(a, b, preferred_element_type=F32)


def together(*arrays):
    return lax.optimization_barrier(arrays)


def grad_tokens():
    y, z, c = (lax.axis_index(a) for a in ("y", "z", "c"))
    r = lax.broadcasted_iota(jnp.int32, (TOKENS, 1), 0)
    early = r < 320
    half = jnp.where(early, r // 160, (r - 320) // 96)
    at = jnp.where(early, r % 160, (r - 320) % 96)
    n, w = at // 32, at % 32
    near = jnp.where(n % 2 == 1, (n + 1) // 2, NZ - n // 2)
    zo = jnp.where(early, near, jnp.where(n == 0, 3, 6 - n))
    yo = 2 * ((half + c) % 2) + w // 16
    return ((y + yo) % NY) * 128 + ((z + zo) % NZ) * 16 + w % 16


def input_tokens():
    x, c = lax.axis_index("x"), lax.axis_index("c")
    r = lax.broadcasted_iota(jnp.int32, (1, TOKENS), 1)
    return 128 * ((x + r // 64) % NX) + 64 * ((c + r // 256) % NC) + r % 64


def order(example_ids):
    rows = grad_tokens()
    pick = rows == input_tokens()
    second = rows >= jnp.sum((example_ids == 0).astype(jnp.int32))
    return jnp.stack([pick & ~second, pick & second]).astype(BF)


def project_kernel(count, core_ref, *refs):
    lhs, q_ref = refs[:count], refs[count]
    mine_ref, other_ref, acc_ref = refs[count + 1 :]
    step = pl.program_id(0)

    @pl.when(step == 0)
    def _():
        acc_ref[...] = jnp.zeros_like(acc_ref)

    for i in range(count):
        acc_ref[i] += dot(lhs[i][...], q_ref[...])

    @pl.when(step == pl.num_programs(0) - 1)
    def _():
        here = pl.multiple_of(core_ref[0] * 32, 32)
        there = pl.multiple_of(32 - core_ref[0] * 32, 32)
        for i in range(count):
            mine_ref[i] = acc_ref[i, pl.ds(here, 32), :]
            other_ref[i] = acc_ref[i, pl.ds(there, 32), :]


def project(chunks, q_grad):
    count, steps = len(chunks), 4
    depth = q_grad.shape[0] // steps
    core = lax.axis_index("c").astype(jnp.int32).reshape(1)
    half = jax.ShapeDtypeStruct((count, 32, ROWS), F32)
    return pl.pallas_call(
        lambda *refs: project_kernel(count, *refs),
        grid_spec=pltpu.PrefetchScalarGridSpec(
            num_scalar_prefetch=1,
            grid=(steps,),
            in_specs=[pl.BlockSpec((64, depth), lambda k, _: (0, k))] * count
            + [pl.BlockSpec((depth, ROWS), lambda k, _: (k, 0))],
            out_specs=[pl.BlockSpec((count, 32, ROWS), lambda k, _: (0, 0, 0))] * 2,
            scratch_shapes=[pltpu.VMEM((count, 64, ROWS), F32)],
        ),
        out_shape=[half, half],
        compiler_params=pltpu.CompilerParams(vmem_limit_bytes=48 * 1024 * 1024),
        cost_estimate=pl.CostEstimate(
            flops=8 * 128 * count * q_grad.size, bytes_accessed=8 * 2 * q_grad.size, transcendentals=0
        ),
    )(core, *chunks, q_grad)


def project_last(chunk, q_grad):
    total = dot(chunk, q_grad).reshape(2, 1, 32, ROWS)
    first = lax.axis_index("c") == 0
    return jnp.where(first, total[0], total[1]), jnp.where(first, total[1], total[0])


def add_core(halves):
    mine, other = halves
    return (mine + shift(other, "c", 1)).reshape(-1, ROWS).astype(BF)


def add_chips(mine):
    part = mine.astype(F32)
    for k in range(1, NX):
        part = part + shift(mine, "x", k).astype(F32)
    return part.astype(BF)


def both(part):
    return jnp.concatenate([part, shift(part, "c", 1)], 0)


def finish_kernel(g_ref, a_ref, eig_ref, out_ref, sum_ref, acc_ref):
    step = pl.program_id(0)

    @pl.when(step == 0)
    def _():
        acc_ref[...] = jnp.zeros_like(acc_ref)

    scale = 1.0 / eig_ref[...].astype(F32)
    for e in range(EXAMPLES):
        blocks = lax.dot_general(g_ref[...], a_ref[e], (((0,), (0,)), ((), ())), preferred_element_type=F32)
        scaled = blocks * scale
        out_ref[e] = scaled.astype(BF)
        acc_ref[e] += (blocks * scaled).reshape(-1, 8, COLS).sum(0)

    @pl.when(step == pl.num_programs(0) - 1)
    def _():
        lanes = acc_ref[...].sum(1)
        sum_ref[...] = sum(lanes[:, 128 * k : 128 * (k + 1)] for k in range(COLS // 128))


def finish(grad_rot, picked, eig_corr):
    tile = ROWS
    return pl.pallas_call(
        finish_kernel,
        grid=(ROWS // tile,),
        in_specs=[
            pl.BlockSpec((TOKENS, tile), lambda i: (0, i)),
            pl.BlockSpec((EXAMPLES, TOKENS, COLS), lambda i: (0, 0, 0)),
            pl.BlockSpec((tile, COLS), lambda i: (i, 0)),
        ],
        out_specs=[
            pl.BlockSpec((EXAMPLES, tile, COLS), lambda i: (0, i, 0)),
            pl.BlockSpec((EXAMPLES, 128), lambda i: (0, 0)),
        ],
        out_shape=[
            jax.ShapeDtypeStruct((EXAMPLES, ROWS, COLS), BF),
            jax.ShapeDtypeStruct((EXAMPLES, 128), F32),
        ],
        scratch_shapes=[pltpu.VMEM((EXAMPLES, 8, COLS), F32)],
        compiler_params=pltpu.CompilerParams(vmem_limit_bytes=48 * 1024 * 1024),
        cost_estimate=pl.CostEstimate(
            flops=4 * TOKENS * ROWS * COLS, bytes_accessed=8 * ROWS * COLS, transcendentals=0
        ),
    )(grad_rot, picked, eig_corr)


def local(grad_out, inputs, q_grad, q_input, eig_corr, example_ids):
    whole = jnp.concatenate([inputs] + [shift(inputs, "x", NX - k) for k in range(1, NX)], 0)
    own = jnp.concatenate([grad_out] + [shift(grad_out, "y", NY - k) for k in range(1, NY)], 0)
    part = dot(both(whole), q_input).astype(BF)
    own, part = together(own, part)

    up, down = shift(own, "z", 1), shift(own, "z", -1)
    part = trade(part.reshape(NY, 128, COLS), "y").astype(F32).sum(0).astype(BF)
    halves0 = project([own], q_grad)
    up, down, part, halves0 = together(up, down, part, halves0)

    up2, down2 = shift(up, "z", 1), shift(down, "z", -1)
    part = trade(part.reshape(NZ, 16, COLS), "z").astype(F32).sum(0).astype(BF)
    halves1 = project([down, up], q_grad)
    mine0 = add_core(halves0)
    up, down, part, mine0, halves1 = together(up2, down2, part, mine0, halves1)

    up2, down2 = shift(up, "z", 1), shift(down, "z", -1)
    part = spread(part, "z", NZ).reshape(128, COLS)
    halves2 = project([down, up], q_grad)
    early = jnp.concatenate([mine0, add_core(halves1)], 0)
    up, down, part, early, halves2 = together(up2, down2, part, early, halves2)

    far = [shift(up[:, :1792], "z", 1), shift(down[:, 1792:], "z", -1)]
    input_rot = spread(part, "y", NY).reshape(TOKENS, COLS)
    halves3 = project([down, up], q_grad)
    mine2 = add_core(halves2)
    early = add_chips(early)
    far, input_rot, early, mine2, halves3 = together(far, input_rot, early, mine2, halves3)

    late = [add_core(halves3), add_core(project_last(jnp.concatenate(far, 1), q_grad))]
    early = both(jnp.concatenate([early, add_chips(mine2)], 0))
    late = both(add_chips(jnp.concatenate(late, 0)))
    rot = [early, late]

    picked = jnp.einsum("ert,ti->eri", order(example_ids), input_rot, preferred_element_type=F32).astype(BF)
    precond, sums = finish(jnp.concatenate(rot, 0), picked, eig_corr)
    sums = spread(sums, ("x", "c"), NX * NC).sum(0)
    sums = spread(sums, ("y", "z"), NY * NZ).sum(0)
    scores = sums.sum(1) / F32(DOUT * DIN)
    return precond, scores


def solution(mesh):
    fine = Mesh(mesh.devices.reshape(NY, NZ, NX, NC), ("y", "z", "x", "c"))
    wide, narrow = ("y", "z"), ("x", "c")
    return jax.shard_map(
        local,
        mesh=fine,
        in_specs=(P(wide, narrow), P(narrow, wide), P(narrow, wide), P(wide, narrow), P(wide, narrow), P()),
        out_specs=(P(None, wide, narrow), P()),
        check_vma=False,
    )
```

```python
import jax
import jax.numpy as jnp
from jax import lax
from jax.experimental import pallas as pl
from jax.experimental.pallas import tpu as pltpu
from jax.sharding import Mesh, PartitionSpec as P

DOUT = 28672
DIN = 8192
EXAMPLES = 2
TOKENS = 512
ROWS, COLS = 896, 1024
NY, NZ, NX, NC = 4, 8, 4, 2
SIZES = {"y": NY, "z": NZ, "x": NX, "c": NC}
BF = jnp.bfloat16
F32 = jnp.float32


def shift(a, axis, k):
    n = SIZES[axis]
    return lax.ppermute(a, axis, [(i, (i + k) % n) for i in range(n)])


def trade(a, axes):
    return lax.all_to_all(a, axes, 0, 0)


def spread(a, axes, n):
    return trade(jnp.broadcast_to(a[None], (n,) + a.shape), axes)


def dot(a, b):
    return jnp.dot(a, b, preferred_element_type=F32)


def together(*arrays):
    return lax.optimization_barrier(arrays)


def grad_tokens():
    y, x, c = (lax.axis_index(a) for a in ("y", "x", "c"))
    r = lax.broadcasted_iota(jnp.int32, (TOKENS, 1), 0)
    z = 4 * ((r // 256 + c) % NC) + (r // 64 + x) % NX
    return ((y + r // 16) % NY) * 128 + z * 16 + r % 16


def input_tokens():
    x, c = lax.axis_index("x"), lax.axis_index("c")
    r = lax.broadcasted_iota(jnp.int32, (1, TOKENS), 1)
    return 128 * ((x + r // 64) % NX) + 64 * ((c + r // 256) % NC) + r % 64


def order(example_ids):
    rows = grad_tokens()
    pick = rows == input_tokens()
    second = rows >= jnp.sum((example_ids == 0).astype(jnp.int32))
    return jnp.stack([pick & ~second, pick & second]).astype(BF)


def both(part):
    return jnp.concatenate([part, shift(part, "c", 1)], 0)


def add_narrow(total):
    x, first = lax.axis_index("x"), lax.axis_index("c") == 0
    total = total.reshape(NC, 256, ROWS)
    mine = jnp.where(first, total[0], total[1])
    other = jnp.where(first, total[1], total[0])
    mine = (mine + shift(other, "c", 1)).astype(BF).reshape(NX, 64, ROWS)
    quarter = [lax.dynamic_index_in_dim(mine, (x + k) % NX, 0, False) for k in range(NX)]
    part = quarter[0].astype(F32)
    for k in range(1, NX):
        part = part + shift(quarter[k], "x", k).astype(F32)
    part = part.astype(BF)
    return both(jnp.concatenate([part] + [shift(part, "x", NX - k) for k in range(1, NX)], 0))


def finish_kernel(g_ref, a_ref, eig_ref, out_ref, sum_ref, acc_ref):
    step = pl.program_id(0)

    @pl.when(step == 0)
    def _():
        acc_ref[...] = jnp.zeros_like(acc_ref)

    scale = 1.0 / eig_ref[...].astype(F32)
    for e in range(EXAMPLES):
        blocks = lax.dot_general(g_ref[...], a_ref[e], (((0,), (0,)), ((), ())), preferred_element_type=F32)
        scaled = blocks * scale
        out_ref[e] = scaled.astype(BF)
        acc_ref[e] += (blocks * scaled).reshape(-1, 8, COLS).sum(0)

    @pl.when(step == pl.num_programs(0) - 1)
    def _():
        lanes = acc_ref[...].sum(1)
        sum_ref[...] = sum(lanes[:, 128 * k : 128 * (k + 1)] for k in range(COLS // 128))


def finish(grad_rot, picked, eig_corr):
    tile = ROWS
    return pl.pallas_call(
        finish_kernel,
        grid=(ROWS // tile,),
        in_specs=[
            pl.BlockSpec((TOKENS, tile), lambda i: (0, i)),
            pl.BlockSpec((EXAMPLES, TOKENS, COLS), lambda i: (0, 0, 0)),
            pl.BlockSpec((tile, COLS), lambda i: (i, 0)),
        ],
        out_specs=[
            pl.BlockSpec((EXAMPLES, tile, COLS), lambda i: (0, i, 0)),
            pl.BlockSpec((EXAMPLES, 128), lambda i: (0, 0)),
        ],
        out_shape=[
            jax.ShapeDtypeStruct((EXAMPLES, ROWS, COLS), BF),
            jax.ShapeDtypeStruct((EXAMPLES, 128), F32),
        ],
        scratch_shapes=[pltpu.VMEM((EXAMPLES, 8, COLS), F32)],
        compiler_params=pltpu.CompilerParams(vmem_limit_bytes=48 * 1024 * 1024),
        cost_estimate=pl.CostEstimate(
            flops=4 * TOKENS * ROWS * COLS, bytes_accessed=8 * ROWS * COLS, transcendentals=0
        ),
    )(grad_rot, picked, eig_corr)


def local(grad_out, inputs, q_grad, q_input, eig_corr, example_ids):
    own = jnp.concatenate([grad_out] + [shift(grad_out, "y", NY - k) for k in range(1, NY)], 0)
    whole = jnp.concatenate([inputs] + [shift(inputs, "x", NX - k) for k in range(1, NX)], 0)
    gathered = lax.all_gather(own, "z", axis=0, tiled=True)

    part = dot(both(whole), q_input).astype(BF)
    part = trade(part.reshape(NY, 128, COLS), "y").astype(F32).sum(0).astype(BF)
    part = trade(part.reshape(NZ, 16, COLS), "z").astype(F32).sum(0).astype(BF)
    part = spread(part, "z", NZ).reshape(128, COLS)
    gathered, part = together(gathered, part)

    input_rot = spread(part, "y", NY).reshape(TOKENS, COLS)
    grad_rot = add_narrow(dot(gathered, q_grad))

    picked = jnp.einsum("ert,ti->eri", order(example_ids), input_rot, preferred_element_type=F32).astype(BF)
    precond, sums = finish(grad_rot, picked, eig_corr)
    sums = spread(sums, ("x", "c"), NX * NC).sum(0)
    sums = spread(sums, ("y", "z"), NY * NZ).sum(0)
    scores = sums.sum(1) / F32(DOUT * DIN)
    return precond, scores


def solution(mesh):
    fine = Mesh(mesh.devices.reshape(NY, NZ, NX, NC), ("y", "z", "x", "c"))
    wide, narrow = ("y", "z"), ("x", "c")
    return jax.shard_map(
        local,
        mesh=fine,
        in_specs=(P(wide, narrow), P(narrow, wide), P(narrow, wide), P(wide, narrow), P(wide, narrow), P()),
        out_specs=(P(None, wide, narrow), P()),
        check_vma=False,
    )
```

```python
import jax
import jax.numpy as jnp
from jax import lax
from jax.experimental import pallas as pl
from jax.experimental.pallas import tpu as pltpu
from jax.sharding import Mesh, PartitionSpec as P

DOUT = 28672
DIN = 8192
EXAMPLES = 2
TOKENS = 512
ROWS, COLS = 896, 1024
NY, NZ, NX, NC = 4, 8, 4, 2
SIZES = {"y": NY, "z": NZ, "x": NX, "c": NC}
BF = jnp.bfloat16
F32 = jnp.float32


def shift(a, axis, k):
    n = SIZES[axis]
    return lax.ppermute(a, axis, [(i, (i + k) % n) for i in range(n)])


def trade(a, axes):
    return lax.all_to_all(a, axes, 0, 0)


def spread(a, axes, n):
    return trade(jnp.broadcast_to(a[None], (n,) + a.shape), axes)


def dot(a, b):
    return jnp.dot(a, b, preferred_element_type=F32)


def together(*arrays):
    return lax.optimization_barrier(arrays)


def grad_tokens():
    y, x, c = (lax.axis_index(a) for a in ("y", "x", "c"))
    r = lax.broadcasted_iota(jnp.int32, (TOKENS, 1), 0)
    z = 4 * ((r // 256 + c) % NC) + (r // 64 + x) % NX
    return ((y + r // 16) % NY) * 128 + z * 16 + r % 16


def input_tokens():
    x, c = lax.axis_index("x"), lax.axis_index("c")
    r = lax.broadcasted_iota(jnp.int32, (1, TOKENS), 1)
    return 128 * ((x + r // 64) % NX) + 64 * ((c + r // 256) % NC) + r % 64


def order(example_ids):
    rows = grad_tokens()
    pick = rows == input_tokens()
    second = rows >= jnp.sum((example_ids == 0).astype(jnp.int32))
    return jnp.stack([pick & ~second, pick & second]).astype(BF)


def both(part):
    return jnp.concatenate([part, shift(part, "c", 1)], 0)


def add_narrow(rows, q_grad):
    x, c = lax.axis_index("x"), lax.axis_index("c")
    other = shift(dot(lax.dynamic_slice_in_dim(rows, 256 - 256 * c, 256), q_grad), "c", 1)
    (mine,) = together(dot(lax.dynamic_slice_in_dim(rows, 256 * c, 256), q_grad))
    mine = (mine + other).astype(BF).reshape(NX, 64, ROWS)
    quarter = [lax.dynamic_index_in_dim(mine, (x + k) % NX, 0, False) for k in range(NX)]
    part = quarter[0].astype(F32)
    for k in range(1, NX):
        part = part + shift(quarter[k], "x", k).astype(F32)
    part = part.astype(BF)
    return both(jnp.concatenate([part] + [shift(part, "x", NX - k) for k in range(1, NX)], 0))


def finish_kernel(g_ref, a_ref, eig_ref, out_ref, sum_ref, acc_ref):
    step = pl.program_id(0)

    @pl.when(step == 0)
    def _():
        acc_ref[...] = jnp.zeros_like(acc_ref)

    scale = 1.0 / eig_ref[...].astype(F32)
    for e in range(EXAMPLES):
        blocks = lax.dot_general(g_ref[...], a_ref[e], (((0,), (0,)), ((), ())), preferred_element_type=F32)
        scaled = blocks * scale
        out_ref[e] = scaled.astype(BF)
        acc_ref[e] += (blocks * scaled).reshape(-1, 8, COLS).sum(0)

    @pl.when(step == pl.num_programs(0) - 1)
    def _():
        lanes = acc_ref[...].sum(1)
        sum_ref[...] = sum(lanes[:, 128 * k : 128 * (k + 1)] for k in range(COLS // 128))


def finish(grad_rot, picked, eig_corr):
    tile = ROWS
    return pl.pallas_call(
        finish_kernel,
        grid=(ROWS // tile,),
        in_specs=[
            pl.BlockSpec((TOKENS, tile), lambda i: (0, i)),
            pl.BlockSpec((EXAMPLES, TOKENS, COLS), lambda i: (0, 0, 0)),
            pl.BlockSpec((tile, COLS), lambda i: (i, 0)),
        ],
        out_specs=[
            pl.BlockSpec((EXAMPLES, tile, COLS), lambda i: (0, i, 0)),
            pl.BlockSpec((EXAMPLES, 128), lambda i: (0, 0)),
        ],
        out_shape=[
            jax.ShapeDtypeStruct((EXAMPLES, ROWS, COLS), BF),
            jax.ShapeDtypeStruct((EXAMPLES, 128), F32),
        ],
        scratch_shapes=[pltpu.VMEM((EXAMPLES, 8, COLS), F32)],
        compiler_params=pltpu.CompilerParams(vmem_limit_bytes=48 * 1024 * 1024),
        cost_estimate=pl.CostEstimate(
            flops=4 * TOKENS * ROWS * COLS, bytes_accessed=8 * ROWS * COLS, transcendentals=0
        ),
    )(grad_rot, picked, eig_corr)


def local(grad_out, inputs, q_grad, q_input, eig_corr, example_ids):
    own = [grad_out] + [shift(grad_out, "y", NY - k) for k in range(1, NY)]
    whole = [inputs] + [shift(inputs, "x", NX - k) for k in range(1, NX)]
    own, whole = together(own, whole)
    gathered = lax.all_gather(jnp.concatenate(own, 0), "z", axis=0, tiled=True)

    part = dot(both(jnp.concatenate(whole, 0)), q_input).astype(BF)
    part = trade(part.reshape(NY, 128, COLS), "y").astype(F32).sum(0).astype(BF)
    part = trade(part.reshape(NZ, 16, COLS), "z").astype(F32).sum(0).astype(BF)
    part = spread(part, "z", NZ).reshape(128, COLS)
    gathered, part = together(gathered, part)

    input_rot = spread(part, "y", NY).reshape(TOKENS, COLS)
    grad_rot = add_narrow(gathered, q_grad)

    picked = jnp.einsum("ert,ti->eri", order(example_ids), input_rot, preferred_element_type=F32).astype(BF)
    precond, sums = finish(grad_rot, picked, eig_corr)
    sums = spread(sums, ("x", "c"), NX * NC).sum(0)
    sums = spread(sums, ("y", "z"), NY * NZ).sum(0)
    scores = sums.sum(1) / F32(DOUT * DIN)
    return precond, scores


def solution(mesh):
    fine = Mesh(mesh.devices.reshape(NY, NZ, NX, NC), ("y", "z", "x", "c"))
    wide, narrow = ("y", "z"), ("x", "c")
    return jax.shard_map(
        local,
        mesh=fine,
        in_specs=(P(wide, narrow), P(narrow, wide), P(narrow, wide), P(wide, narrow), P(wide, narrow), P()),
        out_specs=(P(None, wide, narrow), P()),
        check_vma=False,
    )
```

```python
import jax
import jax.numpy as jnp
from jax import lax
from jax.experimental import pallas as pl
from jax.experimental.pallas import tpu as pltpu
from jax.sharding import Mesh, PartitionSpec as P

DOUT = 28672
DIN = 8192
EXAMPLES = 2
TOKENS = 512
ROWS, COLS = 896, 1024
NY, NZ, NX, NC = 4, 8, 4, 2
SIZES = {"y": NY, "z": NZ, "x": NX, "c": NC}
BF = jnp.bfloat16
F32 = jnp.float32


def shift(a, axis, k):
    n = SIZES[axis]
    return lax.ppermute(a, axis, [(i, (i + k) % n) for i in range(n)])


def trade(a, axes):
    return lax.all_to_all(a, axes, 0, 0)


def spread(a, axes, n):
    return trade(jnp.broadcast_to(a[None], (n,) + a.shape), axes)


def dot(a, b):
    return jnp.dot(a, b, preferred_element_type=F32)


def together(*arrays):
    return lax.optimization_barrier(arrays)


def grad_tokens():
    y, z, c = (lax.axis_index(a) for a in ("y", "z", "c"))
    r = lax.broadcasted_iota(jnp.int32, (TOKENS, 1), 0)
    early = r < 320
    half = jnp.where(early, r // 160, (r - 320) // 96)
    at = jnp.where(early, r % 160, (r - 320) % 96)
    n, w = at // 32, at % 32
    near = jnp.where(n % 2 == 1, (n + 1) // 2, NZ - n // 2)
    zo = jnp.where(early, near, jnp.where(n == 0, 3, 6 - n))
    yo = 2 * ((half + c) % 2) + w // 16
    return ((y + yo) % NY) * 128 + ((z + zo) % NZ) * 16 + w % 16


def input_tokens():
    x, c = lax.axis_index("x"), lax.axis_index("c")
    r = lax.broadcasted_iota(jnp.int32, (1, TOKENS), 1)
    return 128 * ((x + r // 64) % NX) + 64 * ((c + r // 256) % NC) + r % 64


def order(example_ids):
    rows = grad_tokens()
    pick = rows == input_tokens()
    second = rows >= jnp.sum((example_ids == 0).astype(jnp.int32))
    return jnp.stack([pick & ~second, pick & second]).astype(BF)


def project_kernel(count, core_ref, *refs):
    lhs, q_ref = refs[:count], refs[count]
    mine_ref, other_ref, acc_ref = refs[count + 1 :]
    step = pl.program_id(0)

    @pl.when(step == 0)
    def _():
        acc_ref[...] = jnp.zeros_like(acc_ref)

    acc_ref[...] += dot(jnp.concatenate([a[...] for a in lhs], 0), q_ref[...])

    @pl.when(step == pl.num_programs(0) - 1)
    def _():
        for i in range(count):
            here = pl.multiple_of(64 * i + core_ref[0] * 32, 32)
            there = pl.multiple_of(64 * i + 32 - core_ref[0] * 32, 32)
            mine_ref[i] = acc_ref[pl.ds(here, 32), :]
            other_ref[i] = acc_ref[pl.ds(there, 32), :]


def project(chunks, q_grad):
    count, steps = len(chunks), 4
    depth = q_grad.shape[0] // steps
    core = lax.axis_index("c").astype(jnp.int32).reshape(1)
    half = jax.ShapeDtypeStruct((count, 32, ROWS), F32)
    return pl.pallas_call(
        lambda *refs: project_kernel(count, *refs),
        grid_spec=pltpu.PrefetchScalarGridSpec(
            num_scalar_prefetch=1,
            grid=(steps,),
            in_specs=[pl.BlockSpec((64, depth), lambda k, _: (0, k))] * count
            + [pl.BlockSpec((depth, ROWS), lambda k, _: (k, 0))],
            out_specs=[pl.BlockSpec((count, 32, ROWS), lambda k, _: (0, 0, 0))] * 2,
            scratch_shapes=[pltpu.VMEM((count * 64, ROWS), F32)],
        ),
        out_shape=[half, half],
        compiler_params=pltpu.CompilerParams(vmem_limit_bytes=48 * 1024 * 1024),
        cost_estimate=pl.CostEstimate(
            flops=128 * count * q_grad.size, bytes_accessed=4 * q_grad.size, transcendentals=0
        ),
    )(core, *chunks, q_grad)


def project_last(chunk, q_grad):
    total = dot(chunk, q_grad).reshape(2, 1, 32, ROWS)
    first = lax.axis_index("c") == 0
    return jnp.where(first, total[0], total[1]), jnp.where(first, total[1], total[0])


def add_core(halves):
    mine, other = halves
    return (mine + shift(other, "c", 1)).reshape(-1, ROWS).astype(BF)


def add_chips(mine):
    part = mine.astype(F32)
    for k in range(1, NX):
        part = part + shift(mine, "x", k).astype(F32)
    return part.astype(BF)


def both(part):
    return jnp.concatenate([part, shift(part, "c", 1)], 0)


def finish_kernel(g_ref, a_ref, eig_ref, out_ref, sum_ref, acc_ref):
    step = pl.program_id(0)

    @pl.when(step == 0)
    def _():
        acc_ref[...] = jnp.zeros_like(acc_ref)

    scale = 1.0 / eig_ref[...].astype(F32)
    for e in range(EXAMPLES):
        blocks = lax.dot_general(g_ref[...], a_ref[e], (((0,), (0,)), ((), ())), preferred_element_type=F32)
        scaled = blocks * scale
        out_ref[e] = scaled.astype(BF)
        acc_ref[e] += (blocks * scaled).reshape(-1, 8, COLS).sum(0)

    @pl.when(step == pl.num_programs(0) - 1)
    def _():
        lanes = acc_ref[...].sum(1)
        sum_ref[...] = sum(lanes[:, 128 * k : 128 * (k + 1)] for k in range(COLS // 128))


def finish(grad_rot, picked, eig_corr):
    tile = ROWS
    return pl.pallas_call(
        finish_kernel,
        grid=(ROWS // tile,),
        in_specs=[
            pl.BlockSpec((TOKENS, tile), lambda i: (0, i)),
            pl.BlockSpec((EXAMPLES, TOKENS, COLS), lambda i: (0, 0, 0)),
            pl.BlockSpec((tile, COLS), lambda i: (i, 0)),
        ],
        out_specs=[
            pl.BlockSpec((EXAMPLES, tile, COLS), lambda i: (0, i, 0)),
            pl.BlockSpec((EXAMPLES, 128), lambda i: (0, 0)),
        ],
        out_shape=[
            jax.ShapeDtypeStruct((EXAMPLES, ROWS, COLS), BF),
            jax.ShapeDtypeStruct((EXAMPLES, 128), F32),
        ],
        scratch_shapes=[pltpu.VMEM((EXAMPLES, 8, COLS), F32)],
        compiler_params=pltpu.CompilerParams(vmem_limit_bytes=48 * 1024 * 1024),
        cost_estimate=pl.CostEstimate(
            flops=4 * TOKENS * ROWS * COLS, bytes_accessed=8 * ROWS * COLS, transcendentals=0
        ),
    )(grad_rot, picked, eig_corr)


def local(grad_out, inputs, q_grad, q_input, eig_corr, example_ids):
    whole = jnp.concatenate([inputs] + [shift(inputs, "x", NX - k) for k in range(1, NX)], 0)
    own = jnp.concatenate([grad_out] + [shift(grad_out, "y", NY - k) for k in range(1, NY)], 0)
    whole = both(whole)
    own, whole = together(own, whole)

    up, down = shift(own, "z", 1), shift(own, "z", -1)
    part = trade(dot(whole, q_input).astype(BF).reshape(NY, 128, COLS), "y")
    up, down, part = together(up, down, part)

    ring = [own, down, up]
    up, down = shift(up, "z", 1), shift(down, "z", -1)
    part = trade(part.astype(F32).sum(0).astype(BF).reshape(NZ, 16, COLS), "z")
    early = project(ring + [down, up], q_grad)
    up, down, part, early = together(up, down, part, early)

    up, down = shift(up, "z", 1), shift(down, "z", -1)
    part = spread(part.astype(F32).sum(0).astype(BF), "z", NZ).reshape(128, COLS)
    early = add_core(early)
    late = project([down, up], q_grad)
    up, part, early, late = together(up, part, early, late)

    far = shift(up, "z", 1)
    early = add_chips(early)
    late = add_core(late)
    far, early, late = together(far, early, late)

    input_rot = spread(part, "y", NY).reshape(TOKENS, COLS)
    late = jnp.concatenate([late, add_core(project_last(far, q_grad))], 0)
    rot = [both(early), both(add_chips(late))]

    picked = jnp.einsum("ert,ti->eri", order(example_ids), input_rot, preferred_element_type=F32).astype(BF)
    precond, sums = finish(jnp.concatenate(rot, 0), picked, eig_corr)
    sums = spread(sums, ("x", "c"), NX * NC).sum(0)
    sums = spread(sums, ("y", "z"), NY * NZ).sum(0)
    scores = sums.sum(1) / F32(DOUT * DIN)
    return precond, scores


def solution(mesh):
    fine = Mesh(mesh.devices.reshape(NY, NZ, NX, NC), ("y", "z", "x", "c"))
    wide, narrow = ("y", "z"), ("x", "c")
    return jax.shard_map(
        local,
        mesh=fine,
        in_specs=(P(wide, narrow), P(narrow, wide), P(narrow, wide), P(wide, narrow), P(wide, narrow), P()),
        out_specs=(P(None, wide, narrow), P()),
        check_vma=False,
    )
```

```python
import jax
import jax.numpy as jnp
from jax import lax
from jax.experimental import pallas as pl
from jax.experimental.pallas import tpu as pltpu
from jax.sharding import Mesh, PartitionSpec as P

DOUT = 28672
DIN = 8192
EXAMPLES = 2
TOKENS = 512
ROWS, COLS = 896, 1024
NY, NZ, NX, NC = 4, 8, 4, 2
SIZES = {"y": NY, "z": NZ, "x": NX, "c": NC}
BF = jnp.bfloat16
F32 = jnp.float32


def shift(a, axis, k):
    n = SIZES[axis]
    return lax.ppermute(a, axis, [(i, (i + k) % n) for i in range(n)])


def trade(a, axes):
    return lax.all_to_all(a, axes, 0, 0)


def spread(a, axes, n):
    return trade(jnp.broadcast_to(a[None], (n,) + a.shape), axes)


def dot(a, b):
    return jnp.dot(a, b, preferred_element_type=F32)


def together(*arrays):
    return lax.optimization_barrier(arrays)


def grad_tokens():
    y, z, c = (lax.axis_index(a) for a in ("y", "z", "c"))
    r = lax.broadcasted_iota(jnp.int32, (TOKENS, 1), 0)
    early = r < 320
    half = jnp.where(early, r // 160, (r - 320) // 96)
    at = jnp.where(early, r % 160, (r - 320) % 96)
    n, w = at // 32, at % 32
    near = jnp.where(n % 2 == 1, (n + 1) // 2, NZ - n // 2)
    zo = jnp.where(early, near, jnp.where(n == 0, 3, 6 - n))
    yo = 2 * ((half + c) % 2) + w // 16
    return ((y + yo) % NY) * 128 + ((z + zo) % NZ) * 16 + w % 16


def input_tokens():
    x, c = lax.axis_index("x"), lax.axis_index("c")
    r = lax.broadcasted_iota(jnp.int32, (1, TOKENS), 1)
    return 128 * ((x + r // 64) % NX) + 64 * ((c + r // 256) % NC) + r % 64


def order(example_ids):
    rows = grad_tokens()
    pick = rows == input_tokens()
    second = rows >= jnp.sum((example_ids == 0).astype(jnp.int32))
    return jnp.stack([pick & ~second, pick & second]).astype(BF)


def project_kernel(count, core_ref, *refs):
    lhs, q_ref = refs[:count], refs[count]
    mine_ref, other_ref, acc_ref = refs[count + 1 :]
    step = pl.program_id(0)

    @pl.when(step == 0)
    def _():
        acc_ref[...] = jnp.zeros_like(acc_ref)

    acc_ref[...] += dot(jnp.concatenate([a[...] for a in lhs], 0), q_ref[...])

    @pl.when(step == pl.num_programs(0) - 1)
    def _():
        for i in range(count):
            here = pl.multiple_of(64 * i + core_ref[0] * 32, 32)
            there = pl.multiple_of(64 * i + 32 - core_ref[0] * 32, 32)
            mine_ref[i] = acc_ref[pl.ds(here, 32), :]
            other_ref[i] = acc_ref[pl.ds(there, 32), :]


def project(chunks, q_grad):
    count, steps = len(chunks), 4
    depth = q_grad.shape[0] // steps
    core = lax.axis_index("c").astype(jnp.int32).reshape(1)
    half = jax.ShapeDtypeStruct((count, 32, ROWS), F32)
    return pl.pallas_call(
        lambda *refs: project_kernel(count, *refs),
        grid_spec=pltpu.PrefetchScalarGridSpec(
            num_scalar_prefetch=1,
            grid=(steps,),
            in_specs=[pl.BlockSpec((64, depth), lambda k, _: (0, k))] * count
            + [pl.BlockSpec((depth, ROWS), lambda k, _: (k, 0))],
            out_specs=[pl.BlockSpec((count, 32, ROWS), lambda k, _: (0, 0, 0))] * 2,
            scratch_shapes=[pltpu.VMEM((count * 64, ROWS), F32)],
        ),
        out_shape=[half, half],
        compiler_params=pltpu.CompilerParams(vmem_limit_bytes=48 * 1024 * 1024),
        cost_estimate=pl.CostEstimate(
            flops=128 * count * q_grad.size, bytes_accessed=4 * q_grad.size, transcendentals=0
        ),
    )(core, *chunks, q_grad)


def project_last(chunk, q_grad):
    total = dot(chunk, q_grad).reshape(2, 1, 32, ROWS)
    first = lax.axis_index("c") == 0
    return jnp.where(first, total[0], total[1]), jnp.where(first, total[1], total[0])


def add_core(halves):
    mine, other = halves
    return (mine + shift(other, "c", 1)).reshape(-1, ROWS).astype(BF)


def add_chips(mine):
    part = mine.astype(F32)
    for k in range(1, NX):
        part = part + shift(mine, "x", k).astype(F32)
    return part.astype(BF)


def both(part):
    return jnp.concatenate([part, shift(part, "c", 1)], 0)


def finish_kernel(g_ref, a_ref, eig_ref, out_ref, sum_ref, acc_ref):
    step = pl.program_id(0)

    @pl.when(step == 0)
    def _():
        acc_ref[...] = jnp.zeros_like(acc_ref)

    scale = 1.0 / eig_ref[...].astype(F32)
    for e in range(EXAMPLES):
        blocks = lax.dot_general(g_ref[...], a_ref[e], (((0,), (0,)), ((), ())), preferred_element_type=F32)
        scaled = blocks * scale
        out_ref[e] = scaled.astype(BF)
        acc_ref[e] += (blocks * scaled).reshape(-1, 8, COLS).sum(0)

    @pl.when(step == pl.num_programs(0) - 1)
    def _():
        lanes = acc_ref[...].sum(1)
        sum_ref[...] = sum(lanes[:, 128 * k : 128 * (k + 1)] for k in range(COLS // 128))


def finish(grad_rot, picked, eig_corr):
    tile = ROWS
    return pl.pallas_call(
        finish_kernel,
        grid=(ROWS // tile,),
        in_specs=[
            pl.BlockSpec((TOKENS, tile), lambda i: (0, i)),
            pl.BlockSpec((EXAMPLES, TOKENS, COLS), lambda i: (0, 0, 0)),
            pl.BlockSpec((tile, COLS), lambda i: (i, 0)),
        ],
        out_specs=[
            pl.BlockSpec((EXAMPLES, tile, COLS), lambda i: (0, i, 0)),
            pl.BlockSpec((EXAMPLES, 128), lambda i: (0, 0)),
        ],
        out_shape=[
            jax.ShapeDtypeStruct((EXAMPLES, ROWS, COLS), BF),
            jax.ShapeDtypeStruct((EXAMPLES, 128), F32),
        ],
        scratch_shapes=[pltpu.VMEM((EXAMPLES, 8, COLS), F32)],
        compiler_params=pltpu.CompilerParams(vmem_limit_bytes=48 * 1024 * 1024),
        cost_estimate=pl.CostEstimate(
            flops=4 * TOKENS * ROWS * COLS, bytes_accessed=8 * ROWS * COLS, transcendentals=0
        ),
    )(grad_rot, picked, eig_corr)


def local(grad_out, inputs, q_grad, q_input, eig_corr, example_ids):
    whole = jnp.concatenate([inputs] + [shift(inputs, "x", NX - k) for k in range(1, NX)], 0)
    own = jnp.concatenate([grad_out] + [shift(grad_out, "y", NY - k) for k in range(1, NY)], 0)
    part = dot(both(whole), q_input).astype(BF)
    own, part = together(own, part)

    up, down = shift(own, "z", 1), shift(own, "z", -1)
    part = trade(part.reshape(NY, 128, COLS), "y")
    up, down, part = together(up, down, part)

    ring = [own, down, up]
    up, down = shift(up, "z", 1), shift(down, "z", -1)
    part = trade(part.astype(F32).sum(0).astype(BF).reshape(NZ, 16, COLS), "z")
    early = project(ring + [down, up], q_grad)
    up, down, part, early = together(up, down, part, early)

    up, down = shift(up, "z", 1), shift(down, "z", -1)
    part = spread(part.astype(F32).sum(0).astype(BF), "z", NZ).reshape(128, COLS)
    early = add_core(early)
    late = project([down, up], q_grad)
    up, part, early, late = together(up, part, early, late)

    far = project_last(shift(up, "z", 1), q_grad)
    early = add_chips(early)
    late = add_core(late)
    part = spread(part, "y", NY)
    far, part, early, late = together(far, part, early, late)

    input_rot = part.reshape(TOKENS, COLS)
    late = jnp.concatenate([late, add_core(far)], 0)
    rot = [both(early), both(add_chips(late))]

    picked = jnp.einsum("ert,ti->eri", order(example_ids), input_rot, preferred_element_type=F32).astype(BF)
    precond, sums = finish(jnp.concatenate(rot, 0), picked, eig_corr)
    sums = spread(sums, ("x", "c"), NX * NC).sum(0)
    sums = spread(sums, ("y", "z"), NY * NZ).sum(0)
    scores = sums.sum(1) / F32(DOUT * DIN)
    return precond, scores


def solution(mesh):
    fine = Mesh(mesh.devices.reshape(NY, NZ, NX, NC), ("y", "z", "x", "c"))
    wide, narrow = ("y", "z"), ("x", "c")
    return jax.shard_map(
        local,
        mesh=fine,
        in_specs=(P(wide, narrow), P(narrow, wide), P(narrow, wide), P(wide, narrow), P(wide, narrow), P()),
        out_specs=(P(None, wide, narrow), P()),
        check_vma=False,
    )
```

```python
import jax
import jax.numpy as jnp
from jax import lax
from jax.experimental import pallas as pl
from jax.experimental.pallas import tpu as pltpu
from jax.sharding import Mesh, PartitionSpec as P

DOUT = 28672
DIN = 8192
EXAMPLES = 2
TOKENS = 512
ROWS, COLS = 896, 1024
NY, NZ, NX, NC = 4, 8, 4, 2
SIZES = {"y": NY, "z": NZ, "x": NX, "c": NC}
BF = jnp.bfloat16
F32 = jnp.float32


def shift(a, axis, k):
    n = SIZES[axis]
    return lax.ppermute(a, axis, [(i, (i + k) % n) for i in range(n)])


def trade(a, axes):
    return lax.all_to_all(a, axes, 0, 0)


def spread(a, axes, n):
    return trade(jnp.broadcast_to(a[None], (n,) + a.shape), axes)


def dot(a, b):
    return jnp.dot(a, b, preferred_element_type=F32)


def together(*arrays):
    return lax.optimization_barrier(arrays)


def grad_tokens():
    z, c = lax.axis_index("z"), lax.axis_index("c")
    r = lax.broadcasted_iota(jnp.int32, (TOKENS, 1), 0)
    early = r < 320
    half = jnp.where(early, r // 160, (r - 320) // 96)
    at = jnp.where(early, r % 160, (r - 320) % 96)
    n, w = at // 32, at % 32
    near = jnp.where(n % 2 == 1, (n + 1) // 2, NZ - n // 2)
    zo = jnp.where(early, near, jnp.where(n == 0, 3, 6 - n))
    y = 2 * ((half + c) % 2) + w // 16
    return y * 128 + ((z + zo) % NZ) * 16 + w % 16


def input_tokens():
    x, c = lax.axis_index("x"), lax.axis_index("c")
    r = lax.broadcasted_iota(jnp.int32, (1, TOKENS), 1)
    return 128 * ((x + r // 64) % NX) + 64 * ((c + r // 256) % NC) + r % 64


def order(example_ids):
    rows = grad_tokens()
    pick = rows == input_tokens()
    second = rows >= jnp.sum((example_ids == 0).astype(jnp.int32))
    return jnp.stack([pick & ~second, pick & second]).astype(BF)


def project_kernel(count, core_ref, *refs):
    lhs, q_ref = refs[:count], refs[count]
    mine_ref, other_ref, acc_ref = refs[count + 1 :]
    step = pl.program_id(0)

    @pl.when(step == 0)
    def _():
        acc_ref[...] = jnp.zeros_like(acc_ref)

    acc_ref[...] += dot(jnp.concatenate([a[...] for a in lhs], 0), q_ref[...])

    @pl.when(step == pl.num_programs(0) - 1)
    def _():
        for i in range(count):
            here = pl.multiple_of(64 * i + core_ref[0] * 32, 32)
            there = pl.multiple_of(64 * i + 32 - core_ref[0] * 32, 32)
            mine_ref[i] = acc_ref[pl.ds(here, 32), :]
            other_ref[i] = acc_ref[pl.ds(there, 32), :]


def project(chunks, q_grad):
    count, steps = len(chunks), 4
    depth = q_grad.shape[0] // steps
    core = lax.axis_index("c").astype(jnp.int32).reshape(1)
    half = jax.ShapeDtypeStruct((count, 32, ROWS), F32)
    return pl.pallas_call(
        lambda *refs: project_kernel(count, *refs),
        grid_spec=pltpu.PrefetchScalarGridSpec(
            num_scalar_prefetch=1,
            grid=(steps,),
            in_specs=[pl.BlockSpec((64, depth), lambda k, _: (0, k))] * count
            + [pl.BlockSpec((depth, ROWS), lambda k, _: (k, 0))],
            out_specs=[pl.BlockSpec((count, 32, ROWS), lambda k, _: (0, 0, 0))] * 2,
            scratch_shapes=[pltpu.VMEM((count * 64, ROWS), F32)],
        ),
        out_shape=[half, half],
        compiler_params=pltpu.CompilerParams(vmem_limit_bytes=48 * 1024 * 1024),
        cost_estimate=pl.CostEstimate(
            flops=128 * count * q_grad.size, bytes_accessed=4 * q_grad.size, transcendentals=0
        ),
    )(core, *chunks, q_grad)


def project_last(chunk, q_grad):
    total = dot(chunk, q_grad).reshape(2, 1, 32, ROWS)
    first = lax.axis_index("c") == 0
    return jnp.where(first, total[0], total[1]), jnp.where(first, total[1], total[0])


def add_core(halves):
    mine, other = halves
    return (mine + shift(other, "c", 1)).reshape(-1, ROWS).astype(BF)


def add_chips(mine):
    part = mine.astype(F32)
    for k in range(1, NX):
        part = part + shift(mine, "x", k).astype(F32)
    return part.astype(BF)


def both(part):
    return jnp.concatenate([part, shift(part, "c", 1)], 0)


def finish_kernel(g_ref, a_ref, eig_ref, out_ref, sum_ref, acc_ref):
    step = pl.program_id(0)

    @pl.when(step == 0)
    def _():
        acc_ref[...] = jnp.zeros_like(acc_ref)

    scale = 1.0 / eig_ref[...].astype(F32)
    for e in range(EXAMPLES):
        blocks = lax.dot_general(g_ref[...], a_ref[e], (((0,), (0,)), ((), ())), preferred_element_type=F32)
        scaled = blocks * scale
        out_ref[e] = scaled.astype(BF)
        acc_ref[e] += (blocks * scaled).reshape(-1, 8, COLS).sum(0)

    @pl.when(step == pl.num_programs(0) - 1)
    def _():
        lanes = acc_ref[...].sum(1)
        sum_ref[...] = sum(lanes[:, 128 * k : 128 * (k + 1)] for k in range(COLS // 128))


def finish(grad_rot, picked, eig_corr):
    tile = ROWS
    return pl.pallas_call(
        finish_kernel,
        grid=(ROWS // tile,),
        in_specs=[
            pl.BlockSpec((TOKENS, tile), lambda i: (0, i)),
            pl.BlockSpec((EXAMPLES, TOKENS, COLS), lambda i: (0, 0, 0)),
            pl.BlockSpec((tile, COLS), lambda i: (i, 0)),
        ],
        out_specs=[
            pl.BlockSpec((EXAMPLES, tile, COLS), lambda i: (0, i, 0)),
            pl.BlockSpec((EXAMPLES, 128), lambda i: (0, 0)),
        ],
        out_shape=[
            jax.ShapeDtypeStruct((EXAMPLES, ROWS, COLS), BF),
            jax.ShapeDtypeStruct((EXAMPLES, 128), F32),
        ],
        scratch_shapes=[pltpu.VMEM((EXAMPLES, 8, COLS), F32)],
        compiler_params=pltpu.CompilerParams(vmem_limit_bytes=48 * 1024 * 1024),
        cost_estimate=pl.CostEstimate(
            flops=4 * TOKENS * ROWS * COLS, bytes_accessed=8 * ROWS * COLS, transcendentals=0
        ),
    )(grad_rot, picked, eig_corr)


def sum_kernel(pieces_ref, out_ref):
    total = sum(pieces_ref[k].astype(F32) for k in range(pieces_ref.shape[0])).astype(BF)
    for k in range(out_ref.shape[0]):
        out_ref[k] = total


def add_up(pieces, copies):
    return pl.pallas_call(
        sum_kernel,
        out_shape=jax.ShapeDtypeStruct((copies,) + pieces.shape[1:], BF),
        compiler_params=pltpu.CompilerParams(vmem_limit_bytes=8 * 1024 * 1024),
        cost_estimate=pl.CostEstimate(flops=pieces.size, bytes_accessed=2 * pieces.size, transcendentals=0),
    )(pieces)


def local(grad_out, inputs, q_grad, q_input, eig_corr, example_ids):
    whole = jnp.concatenate([inputs] + [shift(inputs, "x", NX - k) for k in range(1, NX)], 0)
    own = spread(grad_out, "y", NY).reshape(64, DOUT // 8)
    part = dot(both(whole), q_input).astype(BF)
    own, part = together(own, part)

    up, down = shift(own, "z", 1), shift(own, "z", -1)
    part = trade(part.reshape(NY, 128, COLS), "y")
    up, down, part = together(up, down, part)

    ring = [own, down, up]
    up, down = shift(up, "z", 1), shift(down, "z", -1)
    part = trade(add_up(part, 1).reshape(NZ, 16, COLS), "z")
    early = project(ring + [down, up], q_grad)
    up, down, part, early = together(up, down, part, early)

    up, down = shift(up, "z", 1), shift(down, "z", -1)
    part = trade(add_up(part, NZ), "z").reshape(128, COLS)
    early = add_core(early)
    late = project([down, up], q_grad)
    up, part, early, late = together(up, part, early, late)

    far = project_last(shift(up, "z", 1), q_grad)
    early = add_chips(early)
    late = add_core(late)
    part = spread(part, "y", NY)
    far, part, early, late = together(far, part, early, late)

    input_rot = part.reshape(TOKENS, COLS)
    late = jnp.concatenate([late, add_core(far)], 0)
    rot = [both(early), both(add_chips(late))]

    picked = jnp.einsum("ert,ti->eri", order(example_ids), input_rot, preferred_element_type=F32).astype(BF)
    precond, sums = finish(jnp.concatenate(rot, 0), picked, eig_corr)
    sums = spread(sums, ("x", "c"), NX * NC).sum(0)
    sums = spread(sums, ("y", "z"), NY * NZ).sum(0)
    scores = sums.sum(1) / F32(DOUT * DIN)
    return precond, scores


def solution(mesh):
    fine = Mesh(mesh.devices.reshape(NY, NZ, NX, NC), ("y", "z", "x", "c"))
    wide, narrow = ("y", "z"), ("x", "c")
    return jax.shard_map(
        local,
        mesh=fine,
        in_specs=(P(wide, narrow), P(narrow, wide), P(narrow, wide), P(wide, narrow), P(wide, narrow), P()),
        out_specs=(P(None, wide, narrow), P()),
        check_vma=False,
    )
```

```python
import jax
import jax.numpy as jnp
from jax import lax
from jax.experimental import pallas as pl
from jax.experimental.pallas import tpu as pltpu
from jax.sharding import Mesh, PartitionSpec as P

DOUT = 28672
DIN = 8192
EXAMPLES = 2
TOKENS = 512
ROWS, COLS = 896, 1024
NY, NZ, NX, NC = 4, 8, 4, 2
SIZES = {"y": NY, "z": NZ, "x": NX, "c": NC}
BF = jnp.bfloat16
F32 = jnp.float32


def shift(a, axis, k):
    n = SIZES[axis]
    return lax.ppermute(a, axis, [(i, (i + k) % n) for i in range(n)])


def trade(a, axes):
    return lax.all_to_all(a, axes, 0, 0)


def spread(a, axes, n):
    return trade(jnp.broadcast_to(a[None], (n,) + a.shape), axes)


def dot(a, b):
    return jnp.dot(a, b, preferred_element_type=F32)


def together(*arrays):
    return lax.optimization_barrier(arrays)


def grad_tokens():
    z, c = lax.axis_index("z"), lax.axis_index("c")
    r = lax.broadcasted_iota(jnp.int32, (TOKENS, 1), 0)
    early = r < 320
    half = jnp.where(early, r // 160, (r - 320) // 96)
    at = jnp.where(early, r % 160, (r - 320) % 96)
    n, w = at // 32, at % 32
    near = jnp.where(n % 2 == 1, (n + 1) // 2, NZ - n // 2)
    zo = jnp.where(early, near, jnp.where(n == 0, 3, 6 - n))
    y = 2 * ((half + c) % 2) + w // 16
    return y * 128 + ((z + zo) % NZ) * 16 + w % 16


def input_tokens():
    x, c = lax.axis_index("x"), lax.axis_index("c")
    r = lax.broadcasted_iota(jnp.int32, (1, TOKENS), 1)
    return 128 * ((x + r // 64) % NX) + 64 * ((c + r // 256) % NC) + r % 64


def order(example_ids):
    rows = grad_tokens()
    pick = rows == input_tokens()
    second = rows >= jnp.sum((example_ids == 0).astype(jnp.int32))
    return jnp.stack([pick & ~second, pick & second]).astype(BF)


def project_kernel(count, core_ref, *refs):
    lhs, q_ref = refs[:count], refs[count]
    mine_ref, other_ref, acc_ref = refs[count + 1 :]
    step = pl.program_id(0)

    @pl.when(step == 0)
    def _():
        acc_ref[...] = jnp.zeros_like(acc_ref)

    acc_ref[...] += dot(jnp.concatenate([a[...] for a in lhs], 0), q_ref[...])

    @pl.when(step == pl.num_programs(0) - 1)
    def _():
        for i in range(count):
            here = pl.multiple_of(64 * i + core_ref[0] * 32, 32)
            there = pl.multiple_of(64 * i + 32 - core_ref[0] * 32, 32)
            mine_ref[i] = acc_ref[pl.ds(here, 32), :]
            other_ref[i] = acc_ref[pl.ds(there, 32), :]


def project(chunks, q_grad):
    count, steps = len(chunks), 4
    depth = q_grad.shape[0] // steps
    core = lax.axis_index("c").astype(jnp.int32).reshape(1)
    half = jax.ShapeDtypeStruct((count, 32, ROWS), F32)
    return pl.pallas_call(
        lambda *refs: project_kernel(count, *refs),
        grid_spec=pltpu.PrefetchScalarGridSpec(
            num_scalar_prefetch=1,
            grid=(steps,),
            in_specs=[pl.BlockSpec((64, depth), lambda k, _: (0, k))] * count
            + [pl.BlockSpec((depth, ROWS), lambda k, _: (k, 0))],
            out_specs=[pl.BlockSpec((count, 32, ROWS), lambda k, _: (0, 0, 0))] * 2,
            scratch_shapes=[pltpu.VMEM((count * 64, ROWS), F32)],
        ),
        out_shape=[half, half],
        compiler_params=pltpu.CompilerParams(vmem_limit_bytes=48 * 1024 * 1024),
        cost_estimate=pl.CostEstimate(
            flops=128 * count * q_grad.size, bytes_accessed=4 * q_grad.size, transcendentals=0
        ),
    )(core, *chunks, q_grad)


def project_last(chunk, q_grad):
    total = dot(chunk, q_grad).reshape(2, 1, 32, ROWS)
    first = lax.axis_index("c") == 0
    return jnp.where(first, total[0], total[1]), jnp.where(first, total[1], total[0])


def add_core(halves):
    mine, other = halves
    return (mine + shift(other, "c", 1)).reshape(-1, ROWS).astype(BF)


def add_chips(mine):
    part = mine.astype(F32)
    for k in range(1, NX):
        part = part + shift(mine, "x", k).astype(F32)
    return part.astype(BF)


def both(part):
    return jnp.concatenate([part, shift(part, "c", 1)], 0)


def score_kernel(g_ref, a_ref, eig_ref, sum_ref):
    scale = 1.0 / eig_ref[...].astype(F32)
    for e in range(EXAMPLES):
        blocks = lax.dot_general(g_ref[...], a_ref[e], (((0,), (0,)), ((), ())), preferred_element_type=F32)
        lanes = (blocks * (blocks * scale)).sum(0, keepdims=True)
        sum_ref[e : e + 1] = sum(lanes[:, 128 * k : 128 * (k + 1)] for k in range(COLS // 128))


def precond_kernel(g_ref, a_ref, eig_ref, out_ref):
    scale = 1.0 / eig_ref[...].astype(F32)
    for e in range(EXAMPLES):
        blocks = lax.dot_general(g_ref[...], a_ref[e], (((0,), (0,)), ((), ())), preferred_element_type=F32)
        out_ref[e] = (blocks * scale).astype(BF)


def finish(kernel, shape, grad_rot, picked, eig_corr):
    return pl.pallas_call(
        kernel,
        out_shape=shape,
        compiler_params=pltpu.CompilerParams(vmem_limit_bytes=48 * 1024 * 1024),
        cost_estimate=pl.CostEstimate(
            flops=4 * TOKENS * ROWS * COLS, bytes_accessed=8 * ROWS * COLS, transcendentals=0
        ),
    )(grad_rot, picked, eig_corr)


def sum_kernel(pieces_ref, out_ref):
    total = sum(pieces_ref[k].astype(F32) for k in range(pieces_ref.shape[0])).astype(BF)
    for k in range(out_ref.shape[0]):
        out_ref[k] = total


def add_up(pieces, copies):
    return pl.pallas_call(
        sum_kernel,
        out_shape=jax.ShapeDtypeStruct((copies,) + pieces.shape[1:], BF),
        compiler_params=pltpu.CompilerParams(vmem_limit_bytes=8 * 1024 * 1024),
        cost_estimate=pl.CostEstimate(flops=pieces.size, bytes_accessed=2 * pieces.size, transcendentals=0),
    )(pieces)


def local(grad_out, inputs, q_grad, q_input, eig_corr, example_ids):
    whole = jnp.concatenate([inputs] + [shift(inputs, "x", NX - k) for k in range(1, NX)], 0)
    own = spread(grad_out, "y", NY).reshape(64, DOUT // 8)
    part = dot(both(whole), q_input).astype(BF)
    own, part, picks = together(own, part, order(example_ids))

    up, down = shift(own, "z", 1), shift(own, "z", -1)
    part = trade(part.reshape(NY, 128, COLS), "y")
    up, down, part = together(up, down, part)

    ring = [own, down, up]
    up, down = shift(up, "z", 1), shift(down, "z", -1)
    part = trade(add_up(part, 1).reshape(NZ, 16, COLS), "z")
    early = project(ring + [down, up], q_grad)
    up, down, part, early = together(up, down, part, early)

    up, down = shift(up, "z", 1), shift(down, "z", -1)
    part = trade(add_up(part, NZ), "z").reshape(128, COLS)
    early = add_core(early)
    late = project([down, up], q_grad)
    up, part, early, late = together(up, part, early, late)

    far = project_last(shift(up, "z", 1), q_grad)
    early = add_chips(early)
    late = add_core(late)
    part = spread(part, "y", NY)
    far, part, early, late = together(far, part, early, late)

    input_rot = part.reshape(TOKENS, COLS)
    late = jnp.concatenate([late, add_core(far)], 0)
    rot = [both(early), both(add_chips(late))]

    picked = jnp.einsum("ert,ti->eri", picks, input_rot, preferred_element_type=F32).astype(BF)
    grad_rot = jnp.concatenate(rot, 0)
    sums = finish(score_kernel, jax.ShapeDtypeStruct((EXAMPLES, 128), F32), grad_rot, picked, eig_corr)
    precond = finish(precond_kernel, jax.ShapeDtypeStruct((EXAMPLES, ROWS, COLS), BF), grad_rot, picked, eig_corr)
    sums = spread(sums, ("x", "c"), NX * NC).sum(0)
    sums = spread(sums, ("y", "z"), NY * NZ).sum(0)
    scores = sums.sum(1) / F32(DOUT * DIN)
    return precond, scores


def solution(mesh):
    fine = Mesh(mesh.devices.reshape(NY, NZ, NX, NC), ("y", "z", "x", "c"))
    wide, narrow = ("y", "z"), ("x", "c")
    return jax.shard_map(
        local,
        mesh=fine,
        in_specs=(P(wide, narrow), P(narrow, wide), P(narrow, wide), P(wide, narrow), P(wide, narrow), P()),
        out_specs=(P(None, wide, narrow), P()),
        check_vma=False,
    )
```

```python
import jax
import jax.numpy as jnp
from jax import lax
from jax.experimental import pallas as pl
from jax.experimental.pallas import tpu as pltpu
from jax.sharding import Mesh, PartitionSpec as P

DOUT = 28672
DIN = 8192
EXAMPLES = 2
TOKENS = 512
ROWS, COLS = 896, 1024
NY, NZ, NX, NC = 4, 8, 4, 2
SIZES = {"y": NY, "z": NZ, "x": NX, "c": NC}
BF = jnp.bfloat16
F32 = jnp.float32


def shift(a, axis, k):
    n = SIZES[axis]
    return lax.ppermute(a, axis, [(i, (i + k) % n) for i in range(n)])


def trade(a, axes):
    return lax.all_to_all(a, axes, 0, 0)


def spread(a, axes, n):
    return trade(jnp.broadcast_to(a[None], (n,) + a.shape), axes)


def dot(a, b):
    return jnp.dot(a, b, preferred_element_type=F32)


def together(*arrays):
    return lax.optimization_barrier(arrays)


def grad_tokens():
    z, c = lax.axis_index("z"), lax.axis_index("c")
    r = lax.broadcasted_iota(jnp.int32, (TOKENS, 1), 0)
    early = r < 320
    half = jnp.where(early, r // 160, (r - 320) // 96)
    at = jnp.where(early, r % 160, (r - 320) % 96)
    n, w = at // 32, at % 32
    near = jnp.where(n % 2 == 1, (n + 1) // 2, NZ - n // 2)
    zo = jnp.where(early, near, jnp.where(n == 0, 3, 6 - n))
    y = 2 * ((half + c) % 2) + w // 16
    return y * 128 + ((z + zo) % NZ) * 16 + w % 16


def input_tokens():
    x, c = lax.axis_index("x"), lax.axis_index("c")
    r = lax.broadcasted_iota(jnp.int32, (1, TOKENS), 1)
    return 128 * ((x + r // 64) % NX) + 64 * ((c + r // 256) % NC) + r % 64


def order(example_ids):
    rows = grad_tokens()
    pick = rows == input_tokens()
    second = rows >= jnp.sum((example_ids == 0).astype(jnp.int32))
    return jnp.stack([pick & ~second, pick & second]).astype(BF)


def project_kernel(count, core_ref, *refs):
    lhs, q_ref = refs[:count], refs[count]
    mine_ref, other_ref, acc_ref = refs[count + 1 :]
    step = pl.program_id(0)

    @pl.when(step == 0)
    def _():
        acc_ref[...] = jnp.zeros_like(acc_ref)

    acc_ref[...] += dot(jnp.concatenate([a[...] for a in lhs], 0), q_ref[...])

    @pl.when(step == pl.num_programs(0) - 1)
    def _():
        for i in range(count):
            here = pl.multiple_of(64 * i + core_ref[0] * 32, 32)
            there = pl.multiple_of(64 * i + 32 - core_ref[0] * 32, 32)
            mine_ref[i] = acc_ref[pl.ds(here, 32), :]
            other_ref[i] = acc_ref[pl.ds(there, 32), :]


def project(chunks, q_grad):
    count, steps = len(chunks), 4
    depth = q_grad.shape[0] // steps
    core = lax.axis_index("c").astype(jnp.int32).reshape(1)
    half = jax.ShapeDtypeStruct((count, 32, ROWS), F32)
    return pl.pallas_call(
        lambda *refs: project_kernel(count, *refs),
        grid_spec=pltpu.PrefetchScalarGridSpec(
            num_scalar_prefetch=1,
            grid=(steps,),
            in_specs=[pl.BlockSpec((64, depth), lambda k, _: (0, k))] * count
            + [pl.BlockSpec((depth, ROWS), lambda k, _: (k, 0))],
            out_specs=[pl.BlockSpec((count, 32, ROWS), lambda k, _: (0, 0, 0))] * 2,
            scratch_shapes=[pltpu.VMEM((count * 64, ROWS), F32)],
        ),
        out_shape=[half, half],
        compiler_params=pltpu.CompilerParams(vmem_limit_bytes=48 * 1024 * 1024),
        cost_estimate=pl.CostEstimate(
            flops=128 * count * q_grad.size, bytes_accessed=4 * q_grad.size, transcendentals=0
        ),
    )(core, *chunks, q_grad)


def project_last(chunk, q_grad):
    total = dot(chunk, q_grad).reshape(2, 1, 32, ROWS)
    first = lax.axis_index("c") == 0
    return jnp.where(first, total[0], total[1]), jnp.where(first, total[1], total[0])


def add_core(halves):
    mine, other = halves
    return (mine + shift(other, "c", 1)).reshape(-1, ROWS).astype(BF)


def add_chips(mine):
    part = mine.astype(F32)
    for k in range(1, NX):
        part = part + shift(mine, "x", k).astype(F32)
    return part.astype(BF)


def both(part):
    return jnp.concatenate([part, shift(part, "c", 1)], 0)


def score_kernel(g_ref, a_ref, eig_ref, sum_ref):
    scale = 1.0 / eig_ref[...].astype(F32)
    for e in range(EXAMPLES):
        blocks = lax.dot_general(g_ref[...], a_ref[e], (((0,), (0,)), ((), ())), preferred_element_type=F32)
        lanes = (blocks * (blocks * scale)).sum(0, keepdims=True)
        sum_ref[e : e + 1] = sum(lanes[:, 128 * k : 128 * (k + 1)] for k in range(COLS // 128))


def precond_kernel(g_ref, a_ref, eig_ref, out_ref):
    scale = 1.0 / eig_ref[...].astype(F32)
    for e in range(EXAMPLES):
        blocks = lax.dot_general(g_ref[...], a_ref[e], (((0,), (0,)), ((), ())), preferred_element_type=F32)
        out_ref[e] = (blocks * scale).astype(BF)


def finish(kernel, shape, grad_rot, picked, eig_corr):
    return pl.pallas_call(
        kernel,
        out_shape=shape,
        compiler_params=pltpu.CompilerParams(vmem_limit_bytes=32 * 1024 * 1024),
        cost_estimate=pl.CostEstimate(
            flops=4 * TOKENS * ROWS * COLS, bytes_accessed=8 * ROWS * COLS, transcendentals=0
        ),
    )(grad_rot, picked, eig_corr)


def sum_kernel(pieces_ref, out_ref):
    total = sum(pieces_ref[k].astype(F32) for k in range(pieces_ref.shape[0])).astype(BF)
    for k in range(out_ref.shape[0]):
        out_ref[k] = total


def add_up(pieces, copies):
    return pl.pallas_call(
        sum_kernel,
        out_shape=jax.ShapeDtypeStruct((copies,) + pieces.shape[1:], BF),
        compiler_params=pltpu.CompilerParams(vmem_limit_bytes=8 * 1024 * 1024),
        cost_estimate=pl.CostEstimate(flops=pieces.size, bytes_accessed=2 * pieces.size, transcendentals=0),
    )(pieces)


def local(grad_out, inputs, q_grad, q_input, eig_corr, example_ids):
    whole = jnp.concatenate([inputs] + [shift(inputs, "x", NX - k) for k in range(1, NX)], 0)
    own = spread(grad_out, "y", NY).reshape(64, DOUT // 8)
    part = dot(both(whole), q_input).astype(BF)
    own, part = together(own, part)

    up, down = shift(own, "z", 1), shift(own, "z", -1)
    part = trade(part.reshape(NY, 128, COLS), "y")
    up, down, part = together(up, down, part)

    ring = [own, down, up]
    up, down = shift(up, "z", 1), shift(down, "z", -1)
    part = trade(add_up(part, 1).reshape(NZ, 16, COLS), "z")
    early = project(ring + [down, up], q_grad)
    up, down, part, early = together(up, down, part, early)

    up, down = shift(up, "z", 1), shift(down, "z", -1)
    part = trade(add_up(part, NZ), "z").reshape(128, COLS)
    early = add_core(early)
    late = project([down, up], q_grad)
    up, part, early, late = together(up, part, early, late)

    far = project_last(shift(up, "z", 1), q_grad)
    early = add_chips(early)
    late = add_core(late)
    part = spread(part, "y", NY)
    far, part, early, late = together(far, part, early, late)

    input_rot = part.reshape(TOKENS, COLS)
    late = jnp.concatenate([late, add_core(far)], 0)
    rot = [both(early), both(add_chips(late))]

    picked = jnp.einsum("ert,ti->eri", order(example_ids), input_rot, preferred_element_type=F32).astype(BF)
    grad_rot = jnp.concatenate(rot, 0)
    sums = finish(score_kernel, jax.ShapeDtypeStruct((EXAMPLES, 128), F32), grad_rot, picked, eig_corr)
    precond = finish(precond_kernel, jax.ShapeDtypeStruct((EXAMPLES, ROWS, COLS), BF), grad_rot, picked, eig_corr)
    sums = spread(sums, ("x", "c"), NX * NC).sum(0)
    sums = spread(sums, ("y", "z"), NY * NZ).sum(0)
    scores = sums.sum(1) / F32(DOUT * DIN)
    return precond, scores


def solution(mesh):
    fine = Mesh(mesh.devices.reshape(NY, NZ, NX, NC), ("y", "z", "x", "c"))
    wide, narrow = ("y", "z"), ("x", "c")
    return jax.shard_map(
        local,
        mesh=fine,
        in_specs=(P(wide, narrow), P(narrow, wide), P(narrow, wide), P(wide, narrow), P(wide, narrow), P()),
        out_specs=(P(None, wide, narrow), P()),
        check_vma=False,
    )
```

```python
import jax
import jax.numpy as jnp
from jax import lax
from jax.experimental import pallas as pl
from jax.experimental.pallas import tpu as pltpu
from jax.sharding import Mesh, PartitionSpec as P

DOUT = 28672
DIN = 8192
EXAMPLES = 2
TOKENS = 512
ROWS, COLS = 896, 1024
NY, NZ, NX, NC = 4, 8, 4, 2
SIZES = {"y": NY, "z": NZ, "x": NX, "c": NC}
BF = jnp.bfloat16
F32 = jnp.float32


def shift(a, axis, k):
    n = SIZES[axis]
    return lax.ppermute(a, axis, [(i, (i + k) % n) for i in range(n)])


def trade(a, axes):
    return lax.all_to_all(a, axes, 0, 0)


def spread(a, axes, n):
    return trade(jnp.broadcast_to(a[None], (n,) + a.shape), axes)


def dot(a, b):
    return jnp.dot(a, b, preferred_element_type=F32)


def together(*arrays):
    return lax.optimization_barrier(arrays)


def grad_tokens():
    y, z, c = (lax.axis_index(a) for a in ("y", "z", "c"))
    r = lax.broadcasted_iota(jnp.int32, (TOKENS, 1), 0)
    early = r < 320
    half = jnp.where(early, r // 160, (r - 320) // 96)
    at = jnp.where(early, r % 160, (r - 320) % 96)
    n, w = at // 32, at % 32
    near = jnp.where(n % 2 == 1, (n + 1) // 2, NZ - n // 2)
    zo = jnp.where(early, near, jnp.where(n == 0, 3, 6 - n))
    yo = 2 * ((half + c) % 2) + w // 16
    return ((y + yo) % NY) * 128 + ((z + zo) % NZ) * 16 + w % 16


def input_tokens():
    x, c = lax.axis_index("x"), lax.axis_index("c")
    r = lax.broadcasted_iota(jnp.int32, (1, TOKENS), 1)
    return 128 * ((x + r // 64) % NX) + 64 * ((c + r // 256) % NC) + r % 64


def order(example_ids):
    rows = grad_tokens()
    pick = rows == input_tokens()
    second = rows >= jnp.sum((example_ids == 0).astype(jnp.int32))
    return jnp.stack([pick & ~second, pick & second]).astype(BF)


def project_kernel(count, core_ref, *refs):
    lhs, q_ref = refs[:count], refs[count]
    mine_ref, other_ref, acc_ref = refs[count + 1 :]
    step = pl.program_id(0)

    @pl.when(step == 0)
    def _():
        acc_ref[...] = jnp.zeros_like(acc_ref)

    acc_ref[...] += dot(jnp.concatenate([a[...] for a in lhs], 0), q_ref[...])

    @pl.when(step == pl.num_programs(0) - 1)
    def _():
        for i in range(count):
            here = pl.multiple_of(64 * i + core_ref[0] * 32, 32)
            there = pl.multiple_of(64 * i + 32 - core_ref[0] * 32, 32)
            mine_ref[i] = acc_ref[pl.ds(here, 32), :]
            other_ref[i] = acc_ref[pl.ds(there, 32), :]


def project(chunks, q_grad):
    count, steps = len(chunks), 4
    depth = q_grad.shape[0] // steps
    core = lax.axis_index("c").astype(jnp.int32).reshape(1)
    half = jax.ShapeDtypeStruct((count, 32, ROWS), F32)
    return pl.pallas_call(
        lambda *refs: project_kernel(count, *refs),
        grid_spec=pltpu.PrefetchScalarGridSpec(
            num_scalar_prefetch=1,
            grid=(steps,),
            in_specs=[pl.BlockSpec((64, depth), lambda k, _: (0, k))] * count
            + [pl.BlockSpec((depth, ROWS), lambda k, _: (k, 0))],
            out_specs=[pl.BlockSpec((count, 32, ROWS), lambda k, _: (0, 0, 0))] * 2,
            scratch_shapes=[pltpu.VMEM((count * 64, ROWS), F32)],
        ),
        out_shape=[half, half],
        compiler_params=pltpu.CompilerParams(vmem_limit_bytes=48 * 1024 * 1024),
        cost_estimate=pl.CostEstimate(
            flops=128 * count * q_grad.size, bytes_accessed=4 * q_grad.size, transcendentals=0
        ),
    )(core, *chunks, q_grad)


def project_last(chunk, q_grad):
    total = dot(chunk, q_grad).reshape(2, 1, 32, ROWS)
    first = lax.axis_index("c") == 0
    return jnp.where(first, total[0], total[1]), jnp.where(first, total[1], total[0])


def add_core(halves):
    mine, other = halves
    return (mine + shift(other, "c", 1)).reshape(-1, ROWS).astype(BF)


def add_chips(mine):
    part = mine.astype(F32)
    for k in range(1, NX):
        part = part + shift(mine, "x", k).astype(F32)
    return part.astype(BF)


def both(part):
    return jnp.concatenate([part, shift(part, "c", 1)], 0)


def finish_kernel(g_ref, a_ref, eig_ref, out_ref, sum_ref, acc_ref):
    step = pl.program_id(0)

    @pl.when(step == 0)
    def _():
        acc_ref[...] = jnp.zeros_like(acc_ref)

    scale = 1.0 / eig_ref[...].astype(F32)
    for e in range(EXAMPLES):
        blocks = lax.dot_general(g_ref[...], a_ref[e], (((0,), (0,)), ((), ())), preferred_element_type=F32)
        scaled = blocks * scale
        out_ref[e] = scaled.astype(BF)
        acc_ref[e] += (blocks * scaled).reshape(-1, 8, COLS).sum(0)

    @pl.when(step == pl.num_programs(0) - 1)
    def _():
        lanes = acc_ref[...].sum(1)
        sum_ref[...] = sum(lanes[:, 128 * k : 128 * (k + 1)] for k in range(COLS // 128))


def finish(grad_rot, picked, eig_corr):
    tile = ROWS
    return pl.pallas_call(
        finish_kernel,
        grid=(ROWS // tile,),
        in_specs=[
            pl.BlockSpec((TOKENS, tile), lambda i: (0, i)),
            pl.BlockSpec((EXAMPLES, TOKENS, COLS), lambda i: (0, 0, 0)),
            pl.BlockSpec((tile, COLS), lambda i: (i, 0)),
        ],
        out_specs=[
            pl.BlockSpec((EXAMPLES, tile, COLS), lambda i: (0, i, 0)),
            pl.BlockSpec((EXAMPLES, 128), lambda i: (0, 0)),
        ],
        out_shape=[
            jax.ShapeDtypeStruct((EXAMPLES, ROWS, COLS), BF),
            jax.ShapeDtypeStruct((EXAMPLES, 128), F32),
        ],
        scratch_shapes=[pltpu.VMEM((EXAMPLES, 8, COLS), F32)],
        compiler_params=pltpu.CompilerParams(vmem_limit_bytes=48 * 1024 * 1024),
        cost_estimate=pl.CostEstimate(
            flops=4 * TOKENS * ROWS * COLS, bytes_accessed=8 * ROWS * COLS, transcendentals=0
        ),
    )(grad_rot, picked, eig_corr)


def sum_kernel(pieces_ref, out_ref):
    total = sum(pieces_ref[k].astype(F32) for k in range(pieces_ref.shape[0])).astype(BF)
    for k in range(out_ref.shape[0]):
        out_ref[k] = total


def add_up(pieces, copies):
    return pl.pallas_call(
        sum_kernel,
        out_shape=jax.ShapeDtypeStruct((copies,) + pieces.shape[1:], BF),
        compiler_params=pltpu.CompilerParams(vmem_limit_bytes=8 * 1024 * 1024),
        cost_estimate=pl.CostEstimate(flops=pieces.size, bytes_accessed=2 * pieces.size, transcendentals=0),
    )(pieces)


def local(grad_out, inputs, q_grad, q_input, eig_corr, example_ids):
    whole = jnp.concatenate([inputs] + [shift(inputs, "x", NX - k) for k in range(1, NX)], 0)
    own = jnp.concatenate([grad_out] + [shift(grad_out, "y", NY - k) for k in range(1, NY)], 0)
    part = dot(both(whole), q_input).astype(BF)
    own, part = together(own, part)

    up, down = shift(own, "z", 1), shift(own, "z", -1)
    part = trade(part.reshape(NY, 128, COLS), "y")
    up, down, part = together(up, down, part)

    ring = [own, down, up]
    up, down = shift(up, "z", 1), shift(down, "z", -1)
    part = trade(add_up(part, 1).reshape(NZ, 16, COLS), "z")
    early = project(ring + [down, up], q_grad)
    up, down, part, early = together(up, down, part, early)

    up, down = shift(up, "z", 1), shift(down, "z", -1)
    part = trade(add_up(part, NZ), "z").reshape(128, COLS)
    early = add_core(early)
    late = project([down, up], q_grad)
    up, part, early, late = together(up, part, early, late)

    far = project_last(shift(up, "z", 1), q_grad)
    early = add_chips(early)
    late = add_core(late)
    part = spread(part, "y", NY)
    far, part, early, late = together(far, part, early, late)

    input_rot = part.reshape(TOKENS, COLS)
    late = jnp.concatenate([late, add_core(far)], 0)
    rot = [both(early), both(add_chips(late))]

    picked = jnp.einsum("ert,ti->eri", order(example_ids), input_rot, preferred_element_type=F32).astype(BF)
    precond, sums = finish(jnp.concatenate(rot, 0), picked, eig_corr)
    sums = spread(sums, ("x", "c"), NX * NC).sum(0)
    sums = spread(sums, ("y", "z"), NY * NZ).sum(0)
    scores = sums.sum(1) / F32(DOUT * DIN)
    return precond, scores


def solution(mesh):
    fine = Mesh(mesh.devices.reshape(NY, NZ, NX, NC), ("y", "z", "x", "c"))
    wide, narrow = ("y", "z"), ("x", "c")
    return jax.shard_map(
        local,
        mesh=fine,
        in_specs=(P(wide, narrow), P(narrow, wide), P(narrow, wide), P(wide, narrow), P(wide, narrow), P()),
        out_specs=(P(None, wide, narrow), P()),
        check_vma=False,
    )
```
